512 devices in a mesh: lat: 16 (over z_hi, x, core), lon: 32 (over z_lo, y).
Axes of the slice: x: 4, y: 4, z: 16 (z_hi: 2, z_lo: 8; z = z_hi * 8 + z_lo), core: 2. Of those that a mesh axis runs over, the one named last changes fastest.
Arguments:
- tokens: bfloat16 [2, 128, 512, 384], P(None, 'lat', 'lon'), may hold values from -6 to 6
- cotangent: bfloat16 [2, 128, 512, 384], P(None, 'lat', 'lon'), may hold values from -6 to 6
- ocean_mask: int32 [16, 64], P(None, 'lon'), may hold values from 0 to 1, as said below
- gain: bfloat16 [384], replicated, may hold values from 0.25 to 1.75
- w_qkv: bfloat16 [384, 1152], replicated, may hold values from -0.3125 to 0.3125
- w_out: bfloat16 [384, 384], replicated, may hold values from -0.3125 to 0.3125
Outputs:
- token_grad: bfloat16 [2, 128, 512, 384], P(None, 'lat', 'lon')
- qkv_grad: bfloat16 [384, 1152], replicated
- out_grad: bfloat16 [384, 384], replicated
- gain_grad: bfloat16 [384], replicated
The draws below stay inside these ranges and needn't reach their ends.
Inputs may be any that keep to these rules, and one draw needn't show every extreme that they name: `ocean_mask`: among the windows of one lon index (all 16 window rows times its 2 window columns) at most 32 are ocean, and the first lon index has exactly that many.
All inputs are finite; a program needn't handle non-finite values.
Results may differ from the reference program's by a relative error of at most 0.014.
Values may be sent and summed in bfloat16 or wider, within the bound.
No kernel may reach another device: no remote copies, remote signals or barrier semaphores. Data moves between devices by JAX's collectives and lax.ppermute only.
A program may use at most 64 MiB of HBM per device.

```python
import jax
import jax.numpy as jnp
from jax import lax

D = 384
HEADS = 12
HDIM = 32
LEVELS = 2
WLAT_DEV = 1
WLON_DEV = 2
CAP = 2
NLAT_W = 16
NLON_W = 64
NLAT = 128
NLON = 512


def draw_ocean_mask(key, part):
    key = jax.random.fold_in(key, 11)
    noise_key, count_key = jax.random.split(key)
    lat_groups = NLAT_W // WLAT_DEV
    groups = NLON_W // WLON_DEV
    group_size = NLAT_W * WLON_DEV
    limit = CAP * lat_groups
    noise = jax.random.randint(noise_key, (NLAT_W, NLON_W), 0, 64)
    lat_pos = jnp.arange(NLAT_W).astype(jnp.int32)
    distance = jnp.abs(2 * lat_pos - (NLAT_W - 1)) * 48 // NLAT_W
    score = noise + distance[:, None]
    score = score.reshape(NLAT_W, groups, WLON_DEV).transpose(1, 0, 2).reshape(groups, group_size)
    score = score * group_size + jnp.arange(group_size).astype(jnp.int32)[None, :]
    order = jnp.argsort(score, axis=1)
    place = jnp.argsort(order, axis=1)
    counts = jax.random.randint(count_key, (groups,), limit // 2, limit + 1)
    counts = jnp.where(jnp.arange(groups) == 0, limit, counts)
    ocean = (place < counts[:, None]).astype(jnp.int32)
    return ocean.reshape(groups, NLAT_W, WLON_DEV).transpose(1, 0, 2).reshape(NLAT_W, NLON_W)


def block_scale(key, shape, cuts, low, largest):
    level = 1.0
    for axis_at, blocks in cuts:
        draws = jax.random.uniform(jax.random.fold_in(jax.random.fold_in(key, 6), axis_at), (blocks,), jnp.float32, low / len(cuts), largest / len(cuts))
        level = level * jnp.repeat(jnp.exp(draws), shape[axis_at] // blocks).reshape((-1,) + (1,) * (len(shape) - 1 - axis_at))
    return level


def bell_draw(stream_key, shape, scale, bound, cuts=(), kind=jnp.bfloat16):
    level = block_scale(stream_key, shape, cuts, -0.22, 0.18) if cuts else 1.0
    values = jax.random.normal(stream_key, shape, jnp.float32) * scale * level
    return jnp.minimum(jnp.maximum(values, -bound), bound).astype(kind)


def setup_inputs(seed: int = 0) -> dict:
    arg_keys = jax.random.split(jax.random.key(seed), 7)
    tokens = bell_draw(arg_keys[0], (LEVELS, NLAT, NLON, D), 1.0, 6.0, ((1, 16), (2, 32)))
    cotangent = bell_draw(arg_keys[1], (LEVELS, NLAT, NLON, D), 1.0, 6.0, ((1, 16), (2, 32)))
    ocean_mask = draw_ocean_mask(jax.random.fold_in(arg_keys[6], 71), 0)
    gain = jnp.clip(1.0 + 0.15 * jax.random.normal(arg_keys[3], (D,), jnp.float32), 0.25, 1.75).astype(jnp.bfloat16)
    w_qkv = bell_draw(arg_keys[4], (D, 3 * D), D ** -0.5, 0.3125)
    w_out = bell_draw(arg_keys[5], (D, D), D ** -0.5, 0.3125)
    return dict(tokens=tokens, cotangent=cotangent, ocean_mask=ocean_mask, gain=gain, w_qkv=w_qkv, w_out=w_out)


def contract(form, left, right):
    return jnp.einsum(form, left.astype(jnp.float32), right.astype(jnp.float32), precision=lax.Precision.HIGHEST)

def window_grads(x_win, g_win, region, gain, w_qkv, w_out):
    count, width, dim = x_win.shape
    scale = HDIM ** (-0.5)
    gain_float32 = gain.astype(jnp.float32)
    x_full = x_win.astype(jnp.float32)
    centered_input = x_full - lax.optimization_barrier(jnp.mean(x_full, -1, keepdims=True))
    inverse_deviation = lax.rsqrt(lax.optimization_barrier(jnp.mean(centered_input * centered_input, -1, keepdims=True)) + 1e-05)
    normalized_input = centered_input * inverse_deviation
    norm_output = (normalized_input * gain_float32).astype(jnp.bfloat16)
    packed = contract('ntd,de->nte', norm_output, w_qkv).astype(jnp.bfloat16)
    packed = packed.reshape(count, width, 3, HEADS, HDIM)
    query = packed[:, :, 0]
    keys = packed[:, :, 1]
    values = packed[:, :, 2]
    scores = contract('nqhc,nkhc->nhqk', query, keys) * scale
    allowed = (region[:, :, None] == region[:, None, :])[:, None]
    scores = jnp.where(allowed, scores, -1e+30)
    expo = jnp.exp(scores - lax.optimization_barrier(jnp.max(scores, -1, keepdims=True)))
    probs = expo / lax.optimization_barrier(jnp.sum(expo, -1, keepdims=True))
    weights = probs.astype(jnp.bfloat16)
    attended = contract('nhqk,nkhc->nqhc', weights, values).astype(jnp.bfloat16).reshape(count, width, dim)
    out_term = contract('ntd,nte->de', attended, g_win)
    d_att = contract('nte,de->ntd', g_win, w_out).astype(jnp.bfloat16).reshape(count, width, HEADS, HDIM)
    d_probs = contract('nqhc,nkhc->nhqk', d_att, values)
    d_values = contract('nhqk,nqhc->nkhc', weights, d_att)
    d_scores = (probs * (d_probs - lax.optimization_barrier(jnp.sum(d_probs * probs, -1, keepdims=True))) * scale).astype(jnp.bfloat16)
    d_query = contract('nhqk,nkhc->nqhc', d_scores, keys)
    d_keys = contract('nhqk,nqhc->nkhc', d_scores, query)
    d_packed = jnp.stack([d_query, d_keys, d_values], 2).reshape(count, width, 3 * dim).astype(jnp.bfloat16)
    qkv_term = contract('ntd,nte->de', norm_output, d_packed)
    gradient_after_norm = contract('nte,de->ntd', d_packed, w_qkv)
    gain_product = lax.optimization_barrier(jnp.sum(gradient_after_norm * normalized_input, (0, 1)))
    normalized_gradient = gradient_after_norm * gain_float32
    branch_gradient = inverse_deviation * (normalized_gradient - lax.optimization_barrier(jnp.mean(normalized_gradient, -1, keepdims=True)) - normalized_input * lax.optimization_barrier(jnp.mean(normalized_gradient * normalized_input, -1, keepdims=True)))
    return (branch_gradient.astype(jnp.bfloat16), qkv_term, out_term, gain_product)

def to_windows(grid):
    levels, rows, cols, dim = grid.shape
    split = grid.reshape(levels, rows // 8, 8, cols // 8, 8, dim)
    return split.transpose(1, 3, 0, 2, 4, 5).reshape(rows // 8, cols // 8, levels * 64, dim)

def from_windows(blocks, levels):
    lat_w, lon_w, width, dim = blocks.shape
    split = blocks.reshape(lat_w, lon_w, levels, 8, 8, dim)
    return split.transpose(2, 0, 3, 1, 4, 5).reshape(levels, lat_w * 8, lon_w * 8, dim)

def reference(tokens, cotangent, ocean_mask, gain, w_qkv, w_out):
    rolled = jnp.roll(tokens, (-4, -4), (1, 2))
    g_rolled = jnp.roll(cotangent, (-4, -4), (1, 2))
    x_blocks = to_windows(rolled)
    g_blocks = to_windows(g_rolled) * ocean_mask[:, :, None, None].astype(jnp.bfloat16)
    width = x_blocks.shape[2]
    token_row = jnp.arange(width) // 8 % 8

    def step(carry, inputs):
        x_row, g_row, lat_index = inputs
        wrapped = (lat_index == NLAT_W - 1) & (token_row >= 4)
        region = jnp.broadcast_to(wrapped.astype(jnp.int32)[None, :], (x_row.shape[0], width))
        branch_gradient, qkv_term, out_term, gain_product = window_grads(x_row, g_row, region, gain, w_qkv, w_out)
        return ((carry[0] + qkv_term, carry[1] + out_term, carry[2] + gain_product), branch_gradient)
    start = (jnp.zeros((D, 3 * D), jnp.float32), jnp.zeros((D, D), jnp.float32), jnp.zeros((D,), jnp.float32))
    sums, d_blocks = lax.scan(step, start, (x_blocks, g_blocks, jnp.arange(NLAT_W).astype(jnp.int32)))
    d_grid = jnp.roll(from_windows(d_blocks, tokens.shape[0]), (4, 4), (1, 2))
    token_grad = (cotangent.astype(jnp.float32) + d_grid.astype(jnp.float32)).astype(jnp.bfloat16)
    return (token_grad, sums[0].astype(jnp.bfloat16), sums[1].astype(jnp.bfloat16), sums[2].astype(jnp.bfloat16))
```

```python
import jax
import jax.numpy as jnp
from jax import lax
from jax.sharding import Mesh
from jax.sharding import PartitionSpec as P

HEADS = 12
HDIM = 32


def passed_along(block, axis, distance):
    devices = range(lax.axis_size(axis))
    route = [((i - distance) % len(devices), i) for i in devices]
    return lax.ppermute(block, axis, route)


def contract(form, left, right):
    return jnp.einsum(form, left, right, preferred_element_type=jnp.float32)


def window_grads(x_win, g_win, region, gain, w_qkv, w_out):
    count, width, dim = x_win.shape
    scale = HDIM ** (-0.5)
    gain_float32 = gain.astype(jnp.float32)
    x_full = x_win.astype(jnp.float32)
    centered_input = x_full - jnp.mean(x_full, -1, keepdims=True)
    inverse_deviation = lax.rsqrt(
        jnp.mean(centered_input * centered_input, -1, keepdims=True) + 1e-05
    )
    normalized_input = centered_input * inverse_deviation
    norm_output = (normalized_input * gain_float32).astype(jnp.bfloat16)
    packed = contract("ntd,de->nte", norm_output, w_qkv).astype(jnp.bfloat16)
    packed = packed.reshape(count, width, 3, HEADS, HDIM)
    query = packed[:, :, 0]
    keys = packed[:, :, 1]
    values = packed[:, :, 2]
    scores = contract("nqhc,nkhc->nhqk", query, keys) * scale
    allowed = (region[:, :, None] == region[:, None, :])[:, None]
    scores = jnp.where(allowed, scores, -1e30)
    expo = jnp.exp(scores - jnp.max(scores, -1, keepdims=True))
    probs = expo / jnp.sum(expo, -1, keepdims=True)
    weights = probs.astype(jnp.bfloat16)
    attended = (
        contract("nhqk,nkhc->nqhc", weights, values).astype(jnp.bfloat16).reshape(count, width, dim)
    )
    out_term = contract("ntd,nte->de", attended, g_win)
    d_att = (
        contract("nte,de->ntd", g_win, w_out)
        .astype(jnp.bfloat16)
        .reshape(count, width, HEADS, HDIM)
    )
    d_probs = contract("nqhc,nkhc->nhqk", d_att, values)
    d_values = contract("nhqk,nqhc->nkhc", weights, d_att)
    d_scores = (probs * (d_probs - jnp.sum(d_probs * probs, -1, keepdims=True)) * scale).astype(
        jnp.bfloat16
    )
    d_query = contract("nhqk,nkhc->nqhc", d_scores, keys)
    d_keys = contract("nhqk,nqhc->nkhc", d_scores, query)
    d_packed = (
        jnp.stack([d_query, d_keys, d_values], 2)
        .reshape(count, width, 3 * dim)
        .astype(jnp.bfloat16)
    )
    qkv_term = contract("ntd,nte->de", norm_output, d_packed)
    gradient_after_norm = contract("nte,de->ntd", d_packed, w_qkv)
    normalized_gradient = gradient_after_norm * gain_float32
    branch_gradient = inverse_deviation * (
        normalized_gradient
        - jnp.mean(normalized_gradient, -1, keepdims=True)
        - normalized_input * jnp.mean(normalized_gradient * normalized_input, -1, keepdims=True)
    )
    return (branch_gradient.astype(jnp.bfloat16), qkv_term, out_term)


def to_windows(grid):
    levels, rows, cols, dim = grid.shape
    split = grid.reshape(levels, rows // 8, 8, cols // 8, 8, dim)
    return split.transpose(1, 3, 0, 2, 4, 5).reshape(rows // 8 * (cols // 8), levels * 64, dim)


def from_windows(blocks, levels, lat_w, lon_w):
    count, width, dim = blocks.shape
    split = blocks.reshape(lat_w, lon_w, levels, 8, 8, dim)
    return split.transpose(2, 0, 3, 1, 4, 5).reshape(levels, lat_w * 8, lon_w * 8, dim)


def edge_lon(stacked, step):
    if step < 0:
        piece = stacked[:, :, :, :4]
    else:
        piece = stacked[:, :, :, -4:]
    moved = passed_along(piece, LON, step)
    if step < 0:
        return jnp.concatenate([stacked[:, :, :, 4:], moved], 3)
    return jnp.concatenate([moved, stacked[:, :, :, :-4]], 3)


def edge_lat(stacked, step):
    if step < 0:
        piece = stacked[:, :, :4]
    else:
        piece = stacked[:, :, -4:]
    moved = passed_along(piece, LAT, step)
    if step < 0:
        return jnp.concatenate([stacked[:, :, 4:], moved], 2)
    return jnp.concatenate([moved, stacked[:, :, :-4]], 2)


LAT = ("zhi", "x", "core")
LON = ("zlo", "y")
PLANE = ("x", "y")
RING = ("zhi", "zlo")


def exchange(parts, axis):
    return lax.all_to_all(parts, axis, 0, 0, tiled=False)


def summed(parts):
    return jnp.sum(parts.astype(jnp.float32), 0).astype(jnp.bfloat16)


def spread(part, axis):
    parts = jnp.broadcast_to(part[None], (lax.axis_size(axis),) + part.shape)
    return exchange(parts, axis)


def reduced(blocks):
    core = lax.axis_index("core")
    swap = [(0, 1), (1, 0)]
    half = blocks.shape[0] // 2
    mine = lax.dynamic_slice_in_dim(blocks, core * half, half, 0)
    other = lax.dynamic_slice_in_dim(blocks, (1 - core) * half, half, 0).astype(jnp.bfloat16)
    mine = (mine + lax.ppermute(other, "core", swap).astype(jnp.float32)).astype(jnp.bfloat16)
    n_plane = lax.axis_size(PLANE)
    mine = summed(exchange(mine.reshape(n_plane, half // n_plane, 128), PLANE))
    n_ring = lax.axis_size(RING)
    mine = summed(exchange(mine.reshape(n_ring, mine.shape[0] // n_ring, 128), RING))
    mine = spread(mine, RING).reshape(-1, 128)
    mine = spread(mine, PLANE).reshape(half, 128)
    other = lax.ppermute(mine, "core", swap)
    first = jnp.where(core == 0, mine, other)
    second = jnp.where(core == 0, other, mine)
    return jnp.concatenate([first, second], 0)


def to_blocks(array):
    rows, cols = array.shape
    return array.reshape(rows, cols // 128, 128).transpose(1, 0, 2).reshape(-1, 128)


def from_blocks(blocks, rows):
    count = blocks.shape[0] // rows
    return blocks.reshape(count, rows, 128).transpose(1, 0, 2).reshape(rows, count * 128)


def local(tokens, cotangent, ocean_mask, gain, w_qkv, w_out):
    levels, rows, cols, dim = tokens.shape
    lat_w = rows // 8
    lon_w = cols // 8
    count = lat_w * lon_w
    n_lat = lax.axis_size(LAT)
    lat_index = lax.axis_index(LAT)
    stacked = edge_lat(edge_lon(jnp.stack([tokens, cotangent]), -1), -1)
    x_blocks = to_windows(stacked[0])
    g_blocks = to_windows(stacked[1])
    width = x_blocks.shape[1]
    token_row = jnp.arange(width) // 8 % 8
    flat = ocean_mask.reshape(-1)
    start = lat_index * count
    local_ocean = lax.dynamic_slice_in_dim(flat, start, count, 0)
    g_masked = g_blocks * local_ocean.astype(jnp.bfloat16)[:, None, None]
    last_window = (lat_index == n_lat - 1) & (jnp.arange(count) // lon_w == lat_w - 1)
    wrapped = last_window[:, None] & (token_row >= 4)[None, :]
    d_blocks, qkv_term, out_term = window_grads(
        x_blocks, g_masked, wrapped.astype(jnp.int32), gain, w_qkv, w_out
    )
    d_grid = from_windows(d_blocks, levels, lat_w, lon_w)
    d_grid = edge_lon(edge_lat(d_grid[None], 1), 1)[0]
    token_grad = (cotangent.astype(jnp.float32) + d_grid.astype(jnp.float32)).astype(jnp.bfloat16)
    blocks = jnp.concatenate([to_blocks(qkv_term), to_blocks(out_term)], 0)
    totals = reduced(blocks)
    qkv_rows = w_qkv.size // 128
    qkv_total = from_blocks(totals[:qkv_rows], dim)
    out_total = from_blocks(totals[qkv_rows:], dim)
    along = jnp.sum(w_qkv.astype(jnp.float32) * qkv_total.astype(jnp.float32), 1)
    gain_total = along / gain.astype(jnp.float32)
    return token_grad, qkv_total, out_total, gain_total.astype(jnp.bfloat16)


def solution(mesh):
    fine = Mesh(mesh.devices.reshape(2, 4, 2, 8, 4), ("zhi", "x", "core", "zlo", "y"))
    return jax.shard_map(
        local,
        mesh=fine,
        in_specs=(
            P(None, LAT, LON, None),
            P(None, LAT, LON, None),
            P(None, LON),
            P(),
            P(),
            P(),
        ),
        out_specs=(P(None, LAT, LON, None), P(), P(), P()),
        check_vma=False,
    )
```

```python
import functools

import jax
import jax.numpy as jnp
import numpy as np
from jax import lax
from jax.experimental import pallas as pl
from jax.experimental.pallas import tpu as pltpu
from jax.sharding import Mesh
from jax.sharding import PartitionSpec as P

HEADS = 12
HDIM = 32
PACK = 4
LANES = 128
WIN = 128
LAT = ("zhi", "x", "core")
LON = ("zlo", "y")
PLANE = ("x", "y")
RING = ("zhi", "zlo")
F32 = jnp.float32
BF16 = jnp.bfloat16


def dot(left, right):
    return jnp.dot(left, right, preferred_element_type=F32)


def dot_nt(left, right):
    return lax.dot_general(left, right, (((1,), (1,)), ((), ())), preferred_element_type=F32)


def call(kernel, outs, *args, scalars=(), scratch=()):
    specs = [pl.BlockSpec(memory_space=pltpu.SMEM)] * len(scalars)
    specs += [pl.BlockSpec(memory_space=pltpu.VMEM)] * len(args)
    return pl.pallas_call(
        kernel,
        out_shape=[jax.ShapeDtypeStruct(s, d) for s, d in outs],
        in_specs=specs,
        out_specs=[pl.BlockSpec(memory_space=pltpu.VMEM)] * len(outs),
        scratch_shapes=scratch,
        compiler_params=pltpu.CompilerParams(vmem_limit_bytes=40 * 1024 * 1024),
    )(*scalars, *args)


def pick_matrix():
    pick = np.zeros((2 * WIN, 320), np.float32)
    for w in range(2):
        for level in range(2):
            for r in range(8):
                for c in range(8):
                    col, row, below = 4 + 8 * w + c, r % 4, r // 4
                    if col < 16:
                        source = 128 * below + level * 64 + row * 16 + col
                    else:
                        source = 256 + 32 * below + level * 16 + row * 4 + col - 16
                    pick[w * WIN + level * 64 + r * 8 + c, source] = 1
    return pick


def corner_matrix():
    corner = np.zeros((32, 128), np.float32)
    for row in range(8):
        for col in range(4):
            corner[row * 4 + col, row * 16 + col] = 1
    return corner


def send_kernel(tok, cot, corner, lat_out, lon_out, diag_out):
    pick = corner[...]
    for i, ref in enumerate((tok, cot)):
        upper = ref[:, 0:4].reshape(WIN, -1)
        lower = ref[:, 4:8].reshape(WIN, -1)
        lat_out[i * WIN : (i + 1) * WIN] = upper
        lon_out[i * 32 : (i + 1) * 32] = dot(pick, lower).astype(BF16)
        diag_out[i * 32 : (i + 1) * 32] = dot(pick, upper).astype(BF16)


def window_kernel(
    meta, tok, cot, lat, lon, diag, pick, put, gain, w_qkv, w_out,
    grads, own_back, lat_back, lon_back, diag_back,
    left, right, packed, d_att,
):
    dim = w_out.shape[0]
    scale = HDIM ** (-0.5)
    gains = gain[...].astype(F32)

    def assembled(i, ref):
        return (
            dot(pick[:, 0:128], ref[:, 4:8].reshape(WIN, dim))
            + dot(pick[:, 128:256], lat[i * WIN : (i + 1) * WIN])
            + dot(pick[:, 256:288], lon[i * 32 : (i + 1) * 32])
            + dot(pick[:, 288:320], diag[i * 32 : (i + 1) * 32])
        )

    x = assembled(0, tok)
    in_first = lax.broadcasted_iota(jnp.int32, (2 * WIN, 1), 0) < WIN
    ocean = jnp.where(in_first, meta[0], meta[1]).astype(F32)
    g = (assembled(1, cot) * ocean).astype(BF16)
    centered = x - jnp.mean(x, -1, keepdims=True)
    rstd = lax.rsqrt(jnp.mean(centered * centered, -1, keepdims=True) + 1e-5)
    xhat = centered * rstd
    normed_full = xhat * gains
    normed = normed_full.astype(BF16)
    left[0] = normed_full.T.astype(BF16)
    packed[...] = dot(normed, w_qkv[...]).astype(BF16)
    d_att[...] = dot_nt(g, w_out[...]).astype(BF16)
    for j in range(dim // LANES):
        right[9 + j] = g[:, j * LANES : (j + 1) * LANES]

    lane = lax.broadcasted_iota(jnp.int32, (1, LANES), 1)
    masks = [(lane // HDIM == h).astype(F32).astype(BF16) for h in range(PACK)]
    key_row = lax.broadcasted_iota(jnp.int32, (WIN, PACK * WIN), 0) // 8 % 8 >= 4
    query_row = lax.broadcasted_iota(jnp.int32, (WIN, PACK * WIN), 1) // 8 % 8 >= 4
    differ = (key_row != query_row).astype(jnp.int32) * meta[2] > 0

    for w in range(2):
        rows = slice(w * WIN, (w + 1) * WIN)
        for group in range(HEADS // PACK):
            cols = [slice(p * dim + group * LANES, p * dim + (group + 1) * LANES) for p in range(3)]
            query, keys, values = packed[rows, cols[0]], packed[rows, cols[1]], packed[rows, cols[2]]
            d_out = d_att[rows, cols[0]]
            query_heads = jnp.concatenate([query * m for m in masks], 0)
            d_out_heads = jnp.concatenate([d_out * m for m in masks], 0)
            scores = jnp.where(differ, -1e30, dot_nt(keys, query_heads) * scale)
            expo = jnp.exp(scores - jnp.max(scores, 0, keepdims=True))
            probs = expo / jnp.sum(expo, 0, keepdims=True)
            weights = probs.astype(BF16)
            d_probs = dot_nt(values, d_out_heads)
            inner = jnp.sum(d_probs * probs, 0, keepdims=True)
            d_scores = (probs * (d_probs - inner) * scale).astype(BF16)
            values_t = values.T
            keys_t = keys.T
            att_t, d_query_t = [], []
            for h in range(PACK):
                span = slice(h * WIN, (h + 1) * WIN)
                feats = slice(h * HDIM, (h + 1) * HDIM)
                att_t.append(dot(values_t[feats], weights[:, span]))
                d_query_t.append(dot(keys_t[feats], d_scores[:, span]))
            att_rows = slice(group * LANES, (group + 1) * LANES)
            left[1, att_rows, rows] = jnp.concatenate(att_t, 0).astype(BF16)
            right[group, rows] = jnp.concatenate(d_query_t, 0).T.astype(BF16)
            right[3 + group, rows] = dot(d_scores, query_heads).astype(BF16)
            right[6 + group, rows] = dot(weights, d_out_heads).astype(BF16)

    for j in range(12):
        half, at = j // 6, j % 6
        slot = lax.rem(half + meta[3], 2)
        term = dot(left[j // 9], right[j])
        grads[slot, at * dim : (at + 1) * dim] = term.astype(BF16)

    d_packed = jnp.concatenate([right[j] for j in range(9)], 1)
    d_normed = dot_nt(d_packed, w_qkv[...])
    d_hat = d_normed * gains
    branch = rstd * (
        d_hat
        - jnp.mean(d_hat, -1, keepdims=True)
        - xhat * jnp.mean(d_hat * xhat, -1, keepdims=True)
    )
    back = dot(put[...], branch.astype(BF16)).astype(BF16)
    own_back[...] = back[0:128]
    lat_back[...] = back[128:256]
    lon_back[...] = back[256:288]
    diag_back[...] = back[288:320]


def token_kernel(cot, own, lat, lon, diag, spread, out):
    fill = spread[...]
    lower = own[...].astype(F32) + dot(fill, lon[...])
    upper = lat[...].astype(F32) + dot(fill, diag[...])
    shape = (2, 4) + cot.shape[2:]
    out[:, 0:4] = (cot[:, 0:4].astype(F32) + upper.reshape(shape)).astype(BF16)
    out[:, 4:8] = (cot[:, 4:8].astype(F32) + lower.reshape(shape)).astype(BF16)


def result_kernel(meta, mine, other, gain, w_qkv, qkv_out, out_out, gain_out):
    dim = out_out.shape[0]

    def write(halves):
        along = jnp.zeros((dim, LANES), F32)
        for j in range(12):
            at = (j % 6) * dim
            block = halves[j // 6][at : at + dim]
            if j < 9:
                cols = slice(j * LANES, (j + 1) * LANES)
                qkv_out[:, cols] = block
                along = along + w_qkv[:, cols].astype(F32) * block.astype(F32)
            else:
                out_out[:, (j - 9) * LANES : (j - 8) * LANES] = block
        total = jnp.sum(along.T, 0, keepdims=True)
        gain_out[...] = (total / gain[...].astype(F32)).astype(BF16)

    @pl.when(meta[3] == 0)
    def _():
        write((mine, other))

    @pl.when(meta[3] != 0)
    def _():
        write((other, mine))


def exchange(parts, axis):
    return lax.all_to_all(parts, axis, 0, 0, tiled=False)


def summed(parts):
    return jnp.sum(parts.astype(F32), 0).astype(BF16)


def spread_along(part, axis):
    parts = jnp.broadcast_to(part[None], (lax.axis_size(axis),) + part.shape)
    return exchange(parts, axis)


def swapped(array):
    return lax.ppermute(array, "core", [(0, 1), (1, 0)])


def reduced(grads):
    half = grads.shape[1]
    mine = (grads[0].astype(F32) + swapped(grads[1]).astype(F32)).astype(BF16)
    mine = summed(exchange(mine.reshape(16, half // 16, LANES), PLANE))
    mine = summed(exchange(mine.reshape(16, half // 256, LANES), RING))
    mine = spread_along(mine, RING).reshape(half // 16, LANES)
    mine = spread_along(mine, PLANE).reshape(half, LANES)
    return mine, swapped(mine)


def local(tokens, cotangent, ocean_mask, gain, w_qkv, w_out):
    dim = w_out.shape[0]
    n_lat, n_lon = lax.axis_size(LAT), lax.axis_size(LON)
    lat_index, core = lax.axis_index(LAT), lax.axis_index("core")
    ocean = lax.dynamic_slice_in_dim(ocean_mask, lat_index, 1, 0).reshape(2)
    flags = jnp.stack([(lat_index == n_lat - 1).astype(jnp.int32), core.astype(jnp.int32)])
    meta = jnp.concatenate([ocean, flags])
    gain_row = gain.reshape(1, dim)
    corner = corner_matrix()
    pick = pick_matrix()
    constant = functools.partial(jnp.asarray, dtype=BF16)

    def from_next(array, axis, size):
        return lax.ppermute(array, axis, [((i + 1) % size, i) for i in range(size)])

    def to_next(array, axis, size):
        return lax.ppermute(array, axis, [(i, (i + 1) % size) for i in range(size)])

    def place_of(a, b):
        return (a % n_lat) * n_lon + b % n_lon

    pairs = [(place_of(a + 1, b + 1), place_of(a, b)) for a in range(n_lat) for b in range(n_lon)]
    send = [((2 * WIN, dim), BF16), ((64, dim), BF16), ((64, dim), BF16)]
    lat, lon, diag = call(send_kernel, send, tokens, cotangent, constant(corner))
    lat = from_next(lat, LAT, n_lat)
    diag = lax.ppermute(diag, LAT + LON, pairs)
    lon = from_next(lon, LON, n_lon)

    backs = [((n, dim), BF16) for n in (WIN, WIN, 32, 32)]
    grads, own_back, lat_back, lon_back, diag_back = call(
        window_kernel, [((2, 6 * dim, LANES), BF16)] + backs,
        tokens, cotangent, lat, lon, diag, constant(pick), constant(pick.T), gain_row, w_qkv, w_out,
        scalars=(meta,),
        scratch=[
            pltpu.VMEM((2, dim, 2 * WIN), BF16),
            pltpu.VMEM((12, 2 * WIN, LANES), BF16),
            pltpu.VMEM((2 * WIN, 3 * dim), BF16),
            pltpu.VMEM((2 * WIN, dim), BF16),
        ],
    )
    lat_back = to_next(lat_back, LAT, n_lat)
    diag_back = lax.ppermute(diag_back, LAT + LON, [(b, a) for a, b in pairs])
    lon_back = to_next(lon_back, LON, n_lon)
    mine, other = reduced(grads)
    (token_grad,) = call(
        token_kernel, [(tokens.shape, BF16)],
        cotangent, own_back, lat_back, lon_back, diag_back, constant(corner.T),
    )
    qkv_grad, out_grad, gain_grad = call(
        result_kernel, [(w_qkv.shape, BF16), (w_out.shape, BF16), ((1, dim), BF16)],
        mine, other, gain_row, w_qkv,
        scalars=(meta,),
    )
    return token_grad, qkv_grad, out_grad, gain_grad.reshape(dim)


def solution(mesh):
    fine = Mesh(mesh.devices.reshape(2, 4, 2, 8, 4), ("zhi", "x", "core", "zlo", "y"))
    tiles = P(None, LAT, LON, None)
    return jax.shard_map(
        local,
        mesh=fine,
        in_specs=(tiles, tiles, P(None, LON), P(), P(), P()),
        out_specs=(tiles, P(), P(), P()),
        check_vma=False,
    )
```

```python
import functools

import jax
import jax.numpy as jnp
import numpy as np
from jax import lax
from jax.experimental import pallas as pl
from jax.experimental.pallas import tpu as pltpu
from jax.sharding import Mesh
from jax.sharding import PartitionSpec as P

HEADS = 12
HDIM = 32
PACK = 4
LANES = 128
WIN = 128
LAT = ("zhi", "x", "core")
LON = ("zlo", "y")
PLANE = ("x", "y")
RING = ("zhi", "zlo")
F32 = jnp.float32
BF16 = jnp.bfloat16


def dot(left, right):
    return jnp.dot(left, right, preferred_element_type=F32)


def dot_nt(left, right):
    return lax.dot_general(left, right, (((1,), (1,)), ((), ())), preferred_element_type=F32)


class Fetch:
    def __init__(self, ref, spot, sem):
        self.spot, self.copy = spot, pltpu.make_async_copy(ref, spot, sem)

    def get(self):
        self.copy.wait()
        return self.spot


def call(kernel, outs, *args, scalars=(), far=(), scratch=()):
    n_scalars, n_far, n_args, n_outs = len(scalars), len(far), len(args), len(outs)

    def body(*refs):
        head, rest = refs[:n_scalars], refs[n_scalars:]
        sources, rest = rest[:n_far], rest[n_far:]
        near, rest = rest[:n_args], rest[n_args:]
        results, rest = rest[:n_outs], rest[n_outs:]
        if not n_far:
            return kernel(*head, *near, *results, *rest)
        spots, sems, own = rest[:n_far], rest[n_far], rest[n_far + 1 :]
        fetches = [Fetch(sources[i], spots[i], sems.at[i]) for i in range(n_far)]
        for fetch in fetches:
            fetch.copy.start()
        kernel(*head, *fetches, *near, *results, *own)

    specs = [pl.BlockSpec(memory_space=pltpu.SMEM)] * n_scalars
    specs += [pl.BlockSpec(memory_space=pl.ANY)] * n_far
    specs += [pl.BlockSpec(memory_space=pltpu.VMEM)] * n_args
    spots = [pltpu.VMEM(a.shape, a.dtype) for a in far]
    if far:
        spots.append(pltpu.SemaphoreType.DMA((n_far,)))
    return pl.pallas_call(
        body,
        out_shape=[jax.ShapeDtypeStruct(s, d) for s, d in outs],
        in_specs=specs,
        out_specs=[pl.BlockSpec(memory_space=pltpu.VMEM)] * n_outs,
        scratch_shapes=spots + list(scratch),
        compiler_params=pltpu.CompilerParams(vmem_limit_bytes=40 * 1024 * 1024),
        name=kernel.__name__,
    )(*scalars, *far, *args)


def pick_matrix():
    pick = np.zeros((2 * WIN, 320), np.float32)
    for w in range(2):
        for level in range(2):
            for r in range(8):
                for c in range(8):
                    col, row, below = 4 + 8 * w + c, r % 4, r // 4
                    if col < 16:
                        source = 128 * below + level * 64 + row * 16 + col
                    else:
                        source = 288 - 32 * below + level * 16 + row * 4 + col - 16
                    pick[w * WIN + level * 64 + r * 8 + c, source] = 1
    return pick


def corner_matrix():
    corner = np.zeros((32, 128), np.float32)
    for row in range(8):
        for col in range(4):
            corner[row * 4 + col, row * 16 + col] = 1
    return corner


def columns_kernel(tok, cot, corner, lon_out, upper_out):
    refs = [tok.get(), cot.get()]
    pick = corner.get()[...]
    for i, ref in enumerate(refs):
        upper = ref[:, 0:4].reshape(WIN, -1)
        lower = ref[:, 4:8].reshape(WIN, -1)
        upper_out[i * WIN : (i + 1) * WIN] = upper
        lon_out[i * 32 : (i + 1) * 32] = dot(pick, upper).astype(BF16)
        lon_out[64 + i * 32 : 64 + (i + 1) * 32] = dot(pick, lower).astype(BF16)


def rows_kernel(upper, lon, lat_out):
    for i in range(2):
        lat_out[i * 160 : i * 160 + WIN] = upper[i * WIN : (i + 1) * WIN]
        lat_out[i * 160 + WIN : (i + 1) * 160] = lon[i * 32 : (i + 1) * 32]


def window_kernel(
    meta, tok, pick, w_qkv, cot, w_out, put, lat, lon, gain,
    grads, own_back, lat_back, side_back,
    left, right, packed, d_att,
):
    dim = lat.shape[1]
    scale = HDIM ** (-0.5)
    gains = gain[...].reshape(1, dim).astype(F32)

    def assembled(i, ref):
        return (
            dot(pick[:, 0:128], ref[:, 4:8].reshape(WIN, dim))
            + dot(pick[:, 128:288], lat[i * 160 : (i + 1) * 160])
            + dot(pick[:, 288:320], lon[64 + i * 32 : 64 + (i + 1) * 32])
        )

    tok, pick = tok.get(), pick.get()
    x = assembled(0, tok)
    in_first = lax.broadcasted_iota(jnp.int32, (2 * WIN, 1), 0) < WIN
    ocean = jnp.where(in_first, meta[0], meta[1]).astype(F32)
    w_qkv, cot, w_out, put = w_qkv.get(), cot.get(), w_out.get(), put.get()
    g = (assembled(1, cot) * ocean).astype(BF16)
    centered = x - jnp.mean(x, -1, keepdims=True)
    rstd = lax.rsqrt(jnp.mean(centered * centered, -1, keepdims=True) + 1e-5)
    xhat = centered * rstd
    normed_full = xhat * gains
    normed = normed_full.astype(BF16)
    left[0] = normed_full.T.astype(BF16)
    packed[...] = dot(normed, w_qkv[...]).astype(BF16)
    d_att[...] = dot_nt(g, w_out[...]).astype(BF16)
    for j in range(dim // LANES):
        right[9 + j] = g[:, j * LANES : (j + 1) * LANES]

    lane = lax.broadcasted_iota(jnp.int32, (1, LANES), 1)
    masks = [(lane // HDIM == h).astype(F32).astype(BF16) for h in range(PACK)]
    key_row = lax.broadcasted_iota(jnp.int32, (WIN, PACK * WIN), 0) // 8 % 8 >= 4
    query_row = lax.broadcasted_iota(jnp.int32, (WIN, PACK * WIN), 1) // 8 % 8 >= 4
    differ = (key_row != query_row).astype(jnp.int32) * meta[2] > 0

    for w in range(2):
        rows = slice(w * WIN, (w + 1) * WIN)
        for group in range(HEADS // PACK):
            cols = [slice(p * dim + group * LANES, p * dim + (group + 1) * LANES) for p in range(3)]
            query, keys, values = packed[rows, cols[0]], packed[rows, cols[1]], packed[rows, cols[2]]
            d_out = d_att[rows, cols[0]]
            query_heads = jnp.concatenate([query * m for m in masks], 0)
            d_out_heads = jnp.concatenate([d_out * m for m in masks], 0)
            scores = jnp.where(differ, -1e30, dot_nt(keys, query_heads) * scale)
            expo = jnp.exp(scores - jnp.max(scores, 0, keepdims=True))
            probs = expo / jnp.sum(expo, 0, keepdims=True)
            weights = probs.astype(BF16)
            d_probs = dot_nt(values, d_out_heads)
            inner = jnp.sum(d_probs * probs, 0, keepdims=True)
            d_scores = (probs * (d_probs - inner) * scale).astype(BF16)
            values_t = values.T
            keys_t = keys.T
            att_t, d_query_t = [], []
            for h in range(PACK):
                span = slice(h * WIN, (h + 1) * WIN)
                feats = slice(h * HDIM, (h + 1) * HDIM)
                att_t.append(dot(values_t[feats], weights[:, span]))
                d_query_t.append(dot(keys_t[feats], d_scores[:, span]))
            att_rows = slice(group * LANES, (group + 1) * LANES)
            left[1, att_rows, rows] = jnp.concatenate(att_t, 0).astype(BF16)
            right[group, rows] = jnp.concatenate(d_query_t, 0).T.astype(BF16)
            right[3 + group, rows] = dot(d_scores, query_heads).astype(BF16)
            right[6 + group, rows] = dot(weights, d_out_heads).astype(BF16)

    for j in range(12):
        half, at = j // 6, j % 6
        slot = lax.rem(half + meta[3], 2)
        term = dot(left[j // 9], right[j])
        grads[slot, at * dim : (at + 1) * dim] = term.astype(BF16)

    d_packed = jnp.concatenate([right[j] for j in range(9)], 1)
    d_normed = dot_nt(d_packed, w_qkv[...])
    d_hat = d_normed * gains
    branch = rstd * (
        d_hat
        - jnp.mean(d_hat, -1, keepdims=True)
        - xhat * jnp.mean(d_hat * xhat, -1, keepdims=True)
    )
    back = dot(put[...], branch.astype(BF16)).astype(BF16)
    own_back[...] = back[0:128]
    lat_back[...] = back[128:256]
    side_back[...] = back[256:320]


def join_kernel(spread, lat_back, side, out):
    fill = spread.get()[...]
    out[...] = (lat_back[...].astype(F32) + dot(fill, side[0:32])).astype(BF16)


def token_kernel(cot, spread, own, lat, side, out):
    cot, fill = cot.get(), spread.get()[...]
    lower = own[...].astype(F32) + dot(fill, side[32:64])
    upper = lat[...].astype(F32)
    shape = (2, 4) + cot.shape[2:]
    out[:, 0:4] = (cot[:, 0:4].astype(F32) + upper.reshape(shape)).astype(BF16)
    out[:, 4:8] = (cot[:, 4:8].astype(F32) + lower.reshape(shape)).astype(BF16)


def result_kernel(meta, w_qkv, mine, other, gain, qkv_out, out_out, gain_out):
    dim = out_out.shape[0]
    w_qkv = w_qkv.get()

    def write(halves):
        along = jnp.zeros((dim, LANES), F32)
        for j in range(12):
            at = (j % 6) * dim
            block = halves[j // 6][at : at + dim]
            if j < 9:
                cols = slice(j * LANES, (j + 1) * LANES)
                qkv_out[:, cols] = block
                along = along + w_qkv[:, cols].astype(F32) * block.astype(F32)
            else:
                out_out[:, (j - 9) * LANES : (j - 8) * LANES] = block
        total = jnp.sum(along.T, 0, keepdims=True)
        gains = gain[...].reshape(1, dim).astype(F32)
        gain_out[...] = (total / gains).astype(BF16).reshape(dim)

    @pl.when(meta[3] == 0)
    def _():
        write((mine, other))

    @pl.when(meta[3] != 0)
    def _():
        write((other, mine))


def exchange(parts, axis):
    return lax.all_to_all(parts, axis, 0, 0, tiled=False)


def summed(parts):
    return jnp.sum(parts.astype(F32), 0).astype(BF16)


def spread_along(part, axis):
    parts = jnp.broadcast_to(part[None], (lax.axis_size(axis),) + part.shape)
    return exchange(parts, axis)


def swapped(array):
    return lax.ppermute(array, "core", [(0, 1), (1, 0)])


def tied(*arrays):
    return lax.optimization_barrier(arrays)


def local(tokens, cotangent, ocean_mask, gain, w_qkv, w_out):
    dim = w_out.shape[0]
    n_lat, n_lon = lax.axis_size(LAT), lax.axis_size(LON)
    lat_index, core = lax.axis_index(LAT), lax.axis_index("core")
    ocean = lax.dynamic_slice_in_dim(ocean_mask, lat_index, 1, 0).reshape(2)
    flags = jnp.stack([(lat_index == n_lat - 1).astype(jnp.int32), core.astype(jnp.int32)])
    meta = jnp.concatenate([ocean, flags])
    corner, pick = corner_matrix(), pick_matrix()
    constant = functools.partial(jnp.asarray, dtype=BF16)

    def from_next(array, axis, size):
        return lax.ppermute(array, axis, [((i + 1) % size, i) for i in range(size)])

    def to_next(array, axis, size):
        return lax.ppermute(array, axis, [(i, (i + 1) % size) for i in range(size)])

    lon, upper = call(
        columns_kernel, [((2 * 64, dim), BF16), ((2 * WIN, dim), BF16)],
        far=(tokens, cotangent, constant(corner)),
    )
    lon = from_next(lon, LON, n_lon)
    (lat,) = call(rows_kernel, [((2 * 160, dim), BF16)], upper, lon)
    lat = from_next(lat, LAT, n_lat)

    half = 6 * dim
    grads, own_back, lat_back, side_back = call(
        window_kernel,
        [((2, half, LANES), BF16), ((WIN, dim), BF16), ((WIN, dim), BF16), ((64, dim), BF16)],
        lat, lon, gain,
        scalars=(meta,),
        far=(tokens, constant(pick), w_qkv, cotangent, w_out, constant(pick.T)),
        scratch=[
            pltpu.VMEM((2, dim, 2 * WIN), BF16),
            pltpu.VMEM((12, 2 * WIN, LANES), BF16),
            pltpu.VMEM((2 * WIN, 3 * dim), BF16),
            pltpu.VMEM((2 * WIN, dim), BF16),
        ],
    )

    side = to_next(side_back, LON, n_lon)
    mine = (grads[0].astype(F32) + swapped(grads[1]).astype(F32)).astype(BF16)
    mine = summed(exchange(mine.reshape(16, half // 16, LANES), PLANE))
    mine, side = tied(mine, side)
    (rows_back,) = call(join_kernel, [((WIN, dim), BF16)], lat_back, side, far=(constant(corner.T),))
    rows_back = to_next(rows_back, LAT, n_lat)
    mine = summed(exchange(mine.reshape(16, half // 256, LANES), RING))
    mine = spread_along(mine, RING).reshape(half // 16, LANES)
    mine, rows_back = tied(mine, rows_back)
    mine = spread_along(mine, PLANE).reshape(half, LANES)
    other = swapped(mine)
    (token_grad,) = call(
        token_kernel, [(tokens.shape, BF16)],
        own_back, rows_back, side,
        far=(cotangent, constant(corner.T)),
    )
    qkv_grad, out_grad, gain_grad = call(
        result_kernel, [(w_qkv.shape, BF16), (w_out.shape, BF16), ((dim,), BF16)],
        mine, other, gain,
        scalars=(meta,), far=(w_qkv,),
    )
    return token_grad, qkv_grad, out_grad, gain_grad


def solution(mesh):
    fine = Mesh(mesh.devices.reshape(2, 4, 2, 8, 4), ("zhi", "x", "core", "zlo", "y"))
    tiles = P(None, LAT, LON, None)
    return jax.shard_map(
        local,
        mesh=fine,
        in_specs=(tiles, tiles, P(None, LON), P(), P(), P()),
        out_specs=(tiles, P(), P(), P()),
        check_vma=False,
    )
```

```python
import functools

import jax
import jax.numpy as jnp
import numpy as np
from jax import lax
from jax.experimental import pallas as pl
from jax.experimental.pallas import tpu as pltpu
from jax.sharding import Mesh
from jax.sharding import PartitionSpec as P

HEADS = 12
HDIM = 32
PACK = 4
LANES = 128
WIN = 128
LAT = ("zhi", "x", "core")
LON = ("zlo", "y")
PLANE = ("x", "y")
RING = ("zhi", "zlo")
F32 = jnp.float32
BF16 = jnp.bfloat16
LONG = 3 * 10**10


def dot(left, right):
    return jnp.dot(left, right, preferred_element_type=F32)


def dot_nt(left, right):
    return lax.dot_general(left, right, (((1,), (1,)), ((), ())), preferred_element_type=F32)


class Fetch:
    def __init__(self, ref, spot, sem):
        self.spot, self.copy = spot, pltpu.make_async_copy(ref, spot, sem)

    def get(self):
        self.copy.wait()
        return self.spot


def call(kernel, outs, *args, scalars=(), far=(), scratch=(), limit=40, flops=0):
    n_scalars, n_far, n_args, n_outs = len(scalars), len(far), len(args), len(outs)

    def body(*refs):
        head, rest = refs[:n_scalars], refs[n_scalars:]
        sources, rest = rest[:n_far], rest[n_far:]
        near, rest = rest[:n_args], rest[n_args:]
        results, rest = rest[:n_outs], rest[n_outs:]
        if not n_far:
            return kernel(*head, *near, *results, *rest)
        spots, sems, own = rest[:n_far], rest[n_far], rest[n_far + 1 :]
        fetches = [Fetch(sources[i], spots[i], sems.at[i]) for i in range(n_far)]
        for fetch in fetches:
            fetch.copy.start()
        kernel(*head, *fetches, *near, *results, *own)

    specs = [pl.BlockSpec(memory_space=pltpu.SMEM)] * n_scalars
    specs += [pl.BlockSpec(memory_space=pltpu.HBM)] * n_far
    specs += [pl.BlockSpec(memory_space=pltpu.VMEM)] * n_args
    spots = [pltpu.VMEM(a.shape, a.dtype) for a in far]
    if far:
        spots.append(pltpu.SemaphoreType.DMA((n_far,)))
    return pl.pallas_call(
        body,
        out_shape=[jax.ShapeDtypeStruct(s, d) for s, d in outs],
        in_specs=specs,
        out_specs=[pl.BlockSpec(memory_space=pltpu.VMEM)] * n_outs,
        scratch_shapes=spots + list(scratch),
        compiler_params=pltpu.CompilerParams(vmem_limit_bytes=limit * 1024 * 1024),
        name=kernel.__name__,
        cost_estimate=pl.CostEstimate(flops=flops, bytes_accessed=0, transcendentals=0) if flops else None,
    )(*scalars, *far, *args)


def pick_matrix():
    pick = np.zeros((2 * WIN, 320), np.float32)
    for w in range(2):
        for level in range(2):
            for r in range(8):
                for c in range(8):
                    col, row, below = 4 + 8 * w + c, r % 4, r // 4
                    if col < 16:
                        source = 128 * below + level * 64 + row * 16 + col
                    else:
                        source = 288 - 32 * below + level * 16 + row * 4 + col - 16
                    pick[w * WIN + level * 64 + r * 8 + c, source] = 1
    return pick


def corner_matrix():
    corner = np.zeros((32, 128), np.float32)
    for row in range(8):
        for col in range(4):
            corner[row * 4 + col, row * 16 + col] = 1
    return corner


def send_kernel(tok, cot, corner, lat_out, diag_out, lon_out):
    refs = [tok.get(), cot.get()]
    pick = corner.get()[...]
    for i, ref in enumerate(refs):
        upper = ref[:, 0:4].reshape(WIN, -1)
        lower = ref[:, 4:8].reshape(WIN, -1)
        lat_out[i * WIN : (i + 1) * WIN] = upper
        diag_out[i * 32 : (i + 1) * 32] = dot(pick, upper).astype(BF16)
        lon_out[i * 32 : (i + 1) * 32] = dot(pick, lower).astype(BF16)


def stage_kernel(*refs):
    half = len(refs) // 2
    for fetch, out in zip(refs[:half], refs[half:]):
        out[...] = fetch.get()[...]


def window_kernel(
    place, ocean_mask, tok, pick, w_qkv, cot, w_out, put, lat, diag, lon, gain,
    grads, own_back, lat_back, side_back,
    left, right, packed, d_att,
):
    dim = lat.shape[1]
    lat_index = place[0]
    core = lax.rem(lat_index, 2)
    last_band = (lat_index == ocean_mask.shape[1] - 1).astype(jnp.int32)
    scale = HDIM ** (-0.5)
    gains = gain[...].reshape(1, dim).astype(F32)

    def assembled(i, ref):
        return (
            dot(pick[:, 0:128], ref[:, 4:8].reshape(WIN, dim))
            + dot(pick[:, 128:256], lat[i * WIN : (i + 1) * WIN])
            + dot(pick[:, 256:288], diag[i * 32 : (i + 1) * 32])
            + dot(pick[:, 288:320], lon[i * 32 : (i + 1) * 32])
        )

    x = assembled(0, tok)
    in_first = lax.broadcasted_iota(jnp.int32, (2 * WIN, 1), 0) < WIN
    ocean = jnp.where(in_first, ocean_mask[0, lat_index], ocean_mask[1, lat_index]).astype(F32)
    g = (assembled(1, cot) * ocean).astype(BF16)
    centered = x - jnp.mean(x, -1, keepdims=True)
    rstd = lax.rsqrt(jnp.mean(centered * centered, -1, keepdims=True) + 1e-5)
    xhat = centered * rstd
    normed_full = xhat * gains
    normed = normed_full.astype(BF16)
    left[0] = normed_full.T.astype(BF16)
    packed[...] = dot(normed, w_qkv[...]).astype(BF16)
    d_att[...] = dot_nt(g, w_out[...]).astype(BF16)
    for j in range(dim // LANES):
        right[9 + j] = g[:, j * LANES : (j + 1) * LANES]

    lane = lax.broadcasted_iota(jnp.int32, (1, LANES), 1)
    masks = [(lane // HDIM == h).astype(F32).astype(BF16) for h in range(PACK)]
    key_row = lax.broadcasted_iota(jnp.int32, (WIN, PACK * WIN), 0) // 8 % 8 >= 4
    query_row = lax.broadcasted_iota(jnp.int32, (WIN, PACK * WIN), 1) // 8 % 8 >= 4
    differ = (key_row != query_row).astype(jnp.int32) * last_band > 0

    for w in range(2):
        rows = slice(w * WIN, (w + 1) * WIN)
        for group in range(HEADS // PACK):
            cols = [slice(p * dim + group * LANES, p * dim + (group + 1) * LANES) for p in range(3)]
            query, keys, values = packed[rows, cols[0]], packed[rows, cols[1]], packed[rows, cols[2]]
            d_out = d_att[rows, cols[0]]
            query_heads = jnp.concatenate([query * m for m in masks], 0)
            d_out_heads = jnp.concatenate([d_out * m for m in masks], 0)
            scores = jnp.where(differ, -1e30, dot_nt(keys, query_heads) * scale)
            expo = jnp.exp(scores - jnp.max(scores, 0, keepdims=True))
            probs = expo / jnp.sum(expo, 0, keepdims=True)
            weights = probs.astype(BF16)
            d_probs = dot_nt(values, d_out_heads)
            inner = jnp.sum(d_probs * probs, 0, keepdims=True)
            d_scores = (probs * (d_probs - inner) * scale).astype(BF16)
            values_t = values.T
            keys_t = keys.T
            att_t, d_query_t = [], []
            for h in range(PACK):
                span = slice(h * WIN, (h + 1) * WIN)
                feats = slice(h * HDIM, (h + 1) * HDIM)
                att_t.append(dot(values_t[feats], weights[:, span]))
                d_query_t.append(dot(keys_t[feats], d_scores[:, span]))
            att_rows = slice(group * LANES, (group + 1) * LANES)
            left[1, att_rows, rows] = jnp.concatenate(att_t, 0).astype(BF16)
            right[group, rows] = jnp.concatenate(d_query_t, 0).T.astype(BF16)
            right[3 + group, rows] = dot(d_scores, query_heads).astype(BF16)
            right[6 + group, rows] = dot(weights, d_out_heads).astype(BF16)

    for j in range(12):
        half, at = j // 6, j % 6
        slot = lax.rem(half + core, 2)
        term = dot(left[j // 9], right[j])
        grads[slot, at * dim : (at + 1) * dim] = term.astype(BF16)

    d_packed = jnp.concatenate([right[j] for j in range(9)], 1)
    d_normed = dot_nt(d_packed, w_qkv[...])
    d_hat = d_normed * gains
    branch = rstd * (
        d_hat
        - jnp.mean(d_hat, -1, keepdims=True)
        - xhat * jnp.mean(d_hat * xhat, -1, keepdims=True)
    )
    back = dot(put[...], branch.astype(BF16)).astype(BF16)
    own_back[...] = back[0:128]
    lat_back[...] = back[128:256]
    side_back[...] = back[256:320]


def join_kernel(spread, lat_back, side, out):
    fill = spread.get()[...]
    out[...] = (lat_back[...].astype(F32) + dot(fill, side[0:32])).astype(BF16)


def token_kernel(cot, spread, own, lat, side, out):
    cot, fill = cot.get(), spread.get()[...]
    lower = own[...].astype(F32) + dot(fill, side[32:64])
    upper = lat[...].astype(F32)
    shape = (2, 4) + cot.shape[2:]
    out[:, 0:4] = (cot[:, 0:4].astype(F32) + upper.reshape(shape)).astype(BF16)
    out[:, 4:8] = (cot[:, 4:8].astype(F32) + lower.reshape(shape)).astype(BF16)


def result_kernel(place, w_qkv, mine, other, gain, qkv_out, out_out, gain_out):
    dim = out_out.shape[0]
    w_qkv = w_qkv.get()

    def write(halves):
        along = jnp.zeros((dim, LANES), F32)
        for j in range(12):
            at = (j % 6) * dim
            block = halves[j // 6][at : at + dim]
            if j < 9:
                cols = slice(j * LANES, (j + 1) * LANES)
                qkv_out[:, cols] = block
                along = along + w_qkv[:, cols].astype(F32) * block.astype(F32)
            else:
                out_out[:, (j - 9) * LANES : (j - 8) * LANES] = block
        total = jnp.sum(along.T, 0, keepdims=True)
        gains = gain[...].reshape(1, dim).astype(F32)
        gain_out[...] = (total / gains).astype(BF16).reshape(dim)

    core = lax.rem(place[0], 2)

    @pl.when(core == 0)
    def _():
        write((mine, other))

    @pl.when(core != 0)
    def _():
        write((other, mine))


def exchange(parts, axis):
    return lax.all_to_all(parts, axis, 0, 0, tiled=False)


def summed(parts):
    return jnp.sum(parts.astype(F32), 0).astype(BF16)


def spread_along(part, axis):
    parts = jnp.broadcast_to(part[None], (lax.axis_size(axis),) + part.shape)
    return exchange(parts, axis)


def swapped(array):
    return lax.ppermute(array, "core", [(0, 1), (1, 0)])


def tied(*arrays):
    return lax.optimization_barrier(arrays)


def local(tokens, cotangent, ocean_mask, gain, w_qkv, w_out):
    dim = w_out.shape[0]
    n_lat, n_lon = lax.axis_size(LAT), lax.axis_size(LON)
    place = lax.axis_index(LAT).astype(jnp.int32).reshape(1)
    corner, pick = corner_matrix(), pick_matrix()
    constant = functools.partial(jnp.asarray, dtype=BF16)

    def from_next(array, axis, size):
        return lax.ppermute(array, axis, [((i + 1) % size, i) for i in range(size)])

    def to_next(array, axis, size):
        return lax.ppermute(array, axis, [(i, (i + 1) % size) for i in range(size)])

    def place_of(a, b):
        return (a % n_lat) * n_lon + b % n_lon

    pairs = [(place_of(a + 1, b + 1), place_of(a, b)) for a in range(n_lat) for b in range(n_lon)]
    lat, diag, lon = call(
        send_kernel, [((2 * WIN, dim), BF16), ((64, dim), BF16), ((64, dim), BF16)],
        far=(tokens, cotangent, constant(corner)), limit=60,
    )
    lat = from_next(lat, LAT, n_lat)
    diag = lax.ppermute(diag, LAT + LON, pairs)
    lon = from_next(lon, LON, n_lon)
    near = (tokens, constant(pick), w_qkv, cotangent, w_out, constant(pick.T))
    near = call(stage_kernel, [(a.shape, BF16) for a in near], far=near)
    half = 6 * dim
    grads, own_back, lat_back, side_back = call(
        window_kernel,
        [((2, half, LANES), BF16), ((WIN, dim), BF16), ((WIN, dim), BF16), ((64, dim), BF16)],
        *near, lat, diag, lon, gain,
        scalars=(place, ocean_mask.T),
        scratch=[
            pltpu.VMEM((2, dim, 2 * WIN), BF16),
            pltpu.VMEM((12, 2 * WIN, LANES), BF16),
            pltpu.VMEM((2 * WIN, 3 * dim), BF16),
            pltpu.VMEM((2 * WIN, dim), BF16),
        ],
    )

    side = to_next(side_back, LON, n_lon)
    mine = (grads[0].astype(F32) + swapped(grads[1]).astype(F32)).astype(BF16)
    mine = summed(exchange(mine.reshape(16, half // 16, LANES), PLANE))
    mine = summed(exchange(mine.reshape(16, half // 256, LANES), RING))
    (rows_back,) = call(
        join_kernel, [((WIN, dim), BF16)], lat_back, side, far=(constant(corner.T),), flops=LONG
    )
    mine, rows_back = tied(mine, rows_back)
    rows_back = to_next(rows_back, LAT, n_lat)
    mine = spread_along(mine, RING).reshape(half // 16, LANES)
    mine = spread_along(mine, PLANE).reshape(half, LANES)
    (token_grad,) = call(
        token_kernel, [(tokens.shape, BF16)],
        own_back, rows_back, side,
        far=(cotangent, constant(corner.T)), flops=LONG,
    )
    mine, token_grad = tied(mine, token_grad)
    other = swapped(mine)
    qkv_grad, out_grad, gain_grad = call(
        result_kernel, [(w_qkv.shape, BF16), (w_out.shape, BF16), ((dim,), BF16)],
        mine, other, gain,
        scalars=(place,), far=(w_qkv,),
    )
    return token_grad, qkv_grad, out_grad, gain_grad


def solution(mesh):
    fine = Mesh(mesh.devices.reshape(2, 4, 2, 8, 4), ("zhi", "x", "core", "zlo", "y"))
    tiles = P(None, LAT, LON, None)
    return jax.shard_map(
        local,
        mesh=fine,
        in_specs=(tiles, tiles, P(None, LON), P(), P(), P()),
        out_specs=(tiles, P(), P(), P()),
        check_vma=False,
    )
```

```python
import functools

import jax
import jax.numpy as jnp
import numpy as np
from jax import lax
from jax.experimental import pallas as pl
from jax.experimental.pallas import tpu as pltpu
from jax.sharding import Mesh
from jax.sharding import PartitionSpec as P

HEADS = 12
HDIM = 32
PACK = 4
LANES = 128
WIN = 128
LAT = ("zhi", "x", "core")
LON = ("zlo", "y")
PLANE = ("x", "y")
RING = ("zhi", "zlo")
F32 = jnp.float32
BF16 = jnp.bfloat16
LONG = 3 * 10**10


def dot(left, right):
    return jnp.dot(left, right, preferred_element_type=F32)


def dot_nt(left, right):
    return lax.dot_general(left, right, (((1,), (1,)), ((), ())), preferred_element_type=F32)


class Fetch:
    def __init__(self, ref, spot, sem):
        self.spot, self.copy = spot, pltpu.make_async_copy(ref, spot, sem)

    def get(self):
        self.copy.wait()
        return self.spot


def call(kernel, outs, *args, scalars=(), far=(), scratch=(), limit=40, flops=0):
    n_scalars, n_far, n_args, n_outs = len(scalars), len(far), len(args), len(outs)

    def body(*refs):
        head, rest = refs[:n_scalars], refs[n_scalars:]
        sources, rest = rest[:n_far], rest[n_far:]
        near, rest = rest[:n_args], rest[n_args:]
        results, rest = rest[:n_outs], rest[n_outs:]
        if not n_far:
            return kernel(*head, *near, *results, *rest)
        spots, sems, own = rest[:n_far], rest[n_far], rest[n_far + 1 :]
        fetches = [Fetch(sources[i], spots[i], sems.at[i]) for i in range(n_far)]
        for fetch in fetches:
            fetch.copy.start()
        kernel(*head, *fetches, *near, *results, *own)

    specs = [pl.BlockSpec(memory_space=pltpu.SMEM)] * n_scalars
    specs += [pl.BlockSpec(memory_space=pltpu.HBM)] * n_far
    specs += [pl.BlockSpec(memory_space=pltpu.VMEM)] * n_args
    spots = [pltpu.VMEM(a.shape, a.dtype) for a in far]
    if far:
        spots.append(pltpu.SemaphoreType.DMA((n_far,)))
    return pl.pallas_call(
        body,
        out_shape=[jax.ShapeDtypeStruct(s, d) for s, d in outs],
        in_specs=specs,
        out_specs=[pl.BlockSpec(memory_space=pltpu.VMEM)] * n_outs,
        scratch_shapes=spots + list(scratch),
        compiler_params=pltpu.CompilerParams(vmem_limit_bytes=limit * 1024 * 1024),
        name=kernel.__name__,
        cost_estimate=pl.CostEstimate(flops=flops, bytes_accessed=0, transcendentals=0) if flops else None,
    )(*scalars, *far, *args)


PICK = (slice(0, 128), slice(128, 224), slice(256, 288), slice(384, 416))
PUT = 256
EDGE_PICK = (slice(256, 384), slice(384, 416))
EDGE_PUT = 384


def constants():
    pick = np.zeros((2 * WIN, 512), np.float32)
    back = np.zeros((288, 2 * WIN), np.float32)
    edge = np.zeros((WIN, 256), np.float32)
    edge_back = np.zeros((160, WIN), np.float32)
    for w in range(2):
        for level in range(2):
            for r in range(8):
                for c in range(8):
                    col, row, below = 4 + 8 * w + c, r % 4, r // 4
                    token = w * WIN + level * 64 + r * 8 + c
                    corner = level * 16 + row * 4 + col - 16
                    grid = level * 64 + row * 16 + col
                    if col >= 16:
                        pick[token, (256 if below else 384) + corner] = 1
                        back[(224 if below else 256) + corner, token] = 1
                    elif below:
                        inner = level * 48 + row * 12 + col - 4
                        pick[token, 128 + inner] = 1
                        back[128 + inner, token] = 1
                    else:
                        pick[token, grid] = 1
                        back[grid, token] = 1
                    if r < 4:
                        token = w * 64 + level * 32 + r * 8 + c
                        edge[token, 128 + corner if col >= 16 else grid] = 1
                        edge_back[128 + corner if col >= 16 else grid, token] = 1
    packed = np.zeros((544, 512), np.float32)
    packed[0:256] = pick
    packed[256:544, 0:256] = back
    packed[256:384, 256:512] = edge
    packed[384:544, 256:384] = edge_back
    return packed


def columns_matrix():
    columns = np.zeros((128, 128), np.float32)
    for row in range(8):
        for col in range(16):
            at = row * 4 + col if col < 4 else 32 + row * 12 + col - 4
            columns[at, row * 16 + col] = 1
    return columns


def send_kernel(tok, cot, columns, lat_out, diag_out, lon_out):
    refs = [tok.get(), cot.get()]
    pick = columns.get()[...]
    for i, ref in enumerate(refs):
        upper = dot(pick, ref[:, 0:4].reshape(WIN, -1)).astype(BF16)
        lower = dot(pick[0:32], ref[:, 4:8].reshape(WIN, -1)).astype(BF16)
        lat_out[i * 96 : (i + 1) * 96] = upper[32:128]
        diag_out[i * 32 : (i + 1) * 32] = upper[0:32]
        lon_out[i * 32 : (i + 1) * 32] = lower
        lon_out[64 + i * 32 : 64 + (i + 1) * 32] = upper[0:32]


def stage_kernel(*refs):
    half = len(refs) // 2
    for fetch, out in zip(refs[:half], refs[half:]):
        out[...] = fetch.get()[...]


def window_kernel(
    place, ocean_mask, tok, const, w_qkv, cot, w_out, lat, diag, lon, gain,
    grads, own_back, lat_back, side_back, edge_back,
    left, right, packed, d_att,
):
    dim = lat.shape[1]
    lat_index = place[0]
    core = lax.rem(lat_index, 2)
    last_band = (lat_index == ocean_mask.shape[1] - 1).astype(jnp.int32)
    scale = HDIM ** (-0.5)
    gains = gain[...].reshape(1, dim).astype(F32)
    lane = lax.broadcasted_iota(jnp.int32, (1, LANES), 1)
    masks = [(lane // HDIM == h).astype(F32).astype(BF16) for h in range(PACK)]
    key_at = lax.broadcasted_iota(jnp.int32, (WIN, PACK * WIN), 0)
    query_at = lax.broadcasted_iota(jnp.int32, (WIN, PACK * WIN), 1) % WIN

    def project(x, g, first):
        rows = slice(first, first + x.shape[0])
        centered = x - jnp.mean(x, -1, keepdims=True)
        rstd = lax.rsqrt(jnp.mean(centered * centered, -1, keepdims=True) + 1e-5)
        xhat = centered * rstd
        normed = xhat * gains
        left[0, :, rows] = normed.T.astype(BF16)
        packed[rows] = dot(normed.astype(BF16), w_qkv[...]).astype(BF16)
        d_att[rows] = dot_nt(g, w_out[...]).astype(BF16)
        for j in range(dim // LANES):
            right[9 + j, rows] = g[:, j * LANES : (j + 1) * LANES]
        return xhat, rstd

    def attend(first, differ):
        rows = slice(first, first + WIN)
        for group in range(HEADS // PACK):
            cols = [slice(p * dim + group * LANES, p * dim + (group + 1) * LANES) for p in range(3)]
            query, keys, values = packed[rows, cols[0]], packed[rows, cols[1]], packed[rows, cols[2]]
            d_out = d_att[rows, cols[0]]
            query_heads = jnp.concatenate([query * m for m in masks], 0)
            d_out_heads = jnp.concatenate([d_out * m for m in masks], 0)
            scores = jnp.where(differ, -1e30, dot_nt(keys, query_heads) * scale)
            expo = jnp.exp(scores - jnp.max(scores, 0, keepdims=True))
            probs = expo / jnp.sum(expo, 0, keepdims=True)
            weights = probs.astype(BF16)
            d_probs = dot_nt(values, d_out_heads)
            inner = jnp.sum(d_probs * probs, 0, keepdims=True)
            d_scores = (probs * (d_probs - inner) * scale).astype(BF16)
            values_t = values.T
            keys_t = keys.T
            att_t, d_query_t = [], []
            for h in range(PACK):
                span = slice(h * WIN, (h + 1) * WIN)
                feats = slice(h * HDIM, (h + 1) * HDIM)
                att_t.append(dot(values_t[feats], weights[:, span]))
                d_query_t.append(dot(keys_t[feats], d_scores[:, span]))
            att_rows = slice(group * LANES, (group + 1) * LANES)
            left[1, att_rows, rows] = jnp.concatenate(att_t, 0).astype(BF16)
            right[group, rows] = jnp.concatenate(d_query_t, 0).T.astype(BF16)
            right[3 + group, rows] = dot(d_scores, query_heads).astype(BF16)
            right[6 + group, rows] = dot(weights, d_out_heads).astype(BF16)

    def branch(first, xhat, rstd):
        rows = slice(first, first + xhat.shape[0])
        d_packed = jnp.concatenate([right[j, rows] for j in range(9)], 1)
        d_normed = dot_nt(d_packed, w_qkv[...])
        d_hat = d_normed * gains
        d_branch = rstd * (
            d_hat
            - jnp.mean(d_hat, -1, keepdims=True)
            - xhat * jnp.mean(d_hat * xhat, -1, keepdims=True)
        )
        return d_branch.astype(BF16)

    def emit(count):
        for j in range(12):
            half, at = j // 6, j % 6
            slot = lax.rem(half + core, 2)
            term = dot(left[j // 9, :, 0:count], right[j, 0:count])
            grads[slot, at * dim : (at + 1) * dim] = term.astype(BF16)

    def assembled(i, ref):
        return (
            dot(const[0:256, PICK[0]], ref[:, 4:8].reshape(WIN, dim))
            + dot(const[0:256, PICK[1]], lat[i * 96 : (i + 1) * 96])
            + dot(const[0:256, PICK[2]], diag[i * 32 : (i + 1) * 32])
            + dot(const[0:256, PICK[3]], lon[i * 32 : (i + 1) * 32])
        )

    def ocean(band, rows, size):
        first = lax.broadcasted_iota(jnp.int32, (rows, 1), 0) < size
        return jnp.where(first, ocean_mask[0, band], ocean_mask[1, band]).astype(F32)

    g = (assembled(1, cot) * ocean(lat_index, 2 * WIN, WIN)).astype(BF16)
    xhat, rstd = project(assembled(0, tok), g, 0)
    lower_differs = ((key_at // 8 % 8 >= 4) != (query_at // 8 % 8 >= 4)).astype(jnp.int32)
    for w in range(2):
        attend(w * WIN, lower_differs * last_band > 0)

    @pl.when(lat_index == 0)
    def _():
        def edge(i, ref):
            return dot(const[256:384, EDGE_PICK[0]], ref[:, 0:4].reshape(WIN, dim)) + dot(
                const[256:384, EDGE_PICK[1]], lon[64 + i * 32 : 64 + (i + 1) * 32]
            )

        last = ocean_mask.shape[1] - 1
        edge_g = (edge(1, cot) * ocean(last, WIN, 64)).astype(BF16)
        edge_xhat, edge_rstd = project(edge(0, tok), edge_g, 2 * WIN)
        attend(2 * WIN, key_at // 64 != query_at // 64)
        edge_branch = branch(2 * WIN, edge_xhat, edge_rstd)
        edge_back[...] = dot(const[EDGE_PUT : EDGE_PUT + 160, 256:384], edge_branch).astype(BF16)
        emit(3 * WIN)

    @pl.when(lat_index != 0)
    def _():
        edge_back[...] = jnp.zeros_like(edge_back)
        emit(2 * WIN)

    back = dot(const[PUT : PUT + 288, 0:256], branch(0, xhat, rstd)).astype(BF16)
    own_back[...] = back[0:128]
    lat_back[...] = back[128:224]
    side_back[0:64] = back[224:288]
    side_back[64:96] = edge_back[128:160]


def join_kernel(lat_back, side, out):
    out[0:96] = lat_back[...]
    out[96:128] = side[0:32]


def token_kernel(cot, spread, own, edge, lat, side, out):
    cot, fill = cot.get(), spread.get()[...]
    lower = own[...].astype(F32) + dot(fill[:, 0:32], side[32:64])
    upper = (
        edge[0:128].astype(F32)
        + dot(fill[:, 0:32], lat[96:128] + side[64:96])
        + dot(fill[:, 128:224], lat[0:96])
    )
    shape = (2, 4) + cot.shape[2:]
    out[:, 0:4] = (cot[:, 0:4].astype(F32) + upper.reshape(shape)).astype(BF16)
    out[:, 4:8] = (cot[:, 4:8].astype(F32) + lower.reshape(shape)).astype(BF16)


def result_kernel(place, w_qkv, mine, other, gain, qkv_out, out_out, gain_out):
    dim = out_out.shape[0]
    w_qkv = w_qkv.get()

    def write(halves):
        along = jnp.zeros((dim, LANES), F32)
        for j in range(12):
            at = (j % 6) * dim
            block = halves[j // 6][at : at + dim]
            if j < 9:
                cols = slice(j * LANES, (j + 1) * LANES)
                qkv_out[:, cols] = block
                along = along + w_qkv[:, cols].astype(F32) * block.astype(F32)
            else:
                out_out[:, (j - 9) * LANES : (j - 8) * LANES] = block
        total = jnp.sum(along.T, 0, keepdims=True)
        gains = gain[...].reshape(1, dim).astype(F32)
        gain_out[...] = (total / gains).astype(BF16).reshape(dim)

    core = lax.rem(place[0], 2)

    @pl.when(core == 0)
    def _():
        write((mine, other))

    @pl.when(core != 0)
    def _():
        write((other, mine))


def exchange(parts, axis):
    return lax.all_to_all(parts, axis, 0, 0, tiled=False)


def summed(parts):
    return jnp.sum(parts.astype(F32), 0).astype(BF16)


def spread_along(part, axis):
    parts = jnp.broadcast_to(part[None], (lax.axis_size(axis),) + part.shape)
    return exchange(parts, axis)


def swapped(array):
    return lax.ppermute(array, "core", [(0, 1), (1, 0)])


def tied(*arrays):
    return lax.optimization_barrier(arrays)


def local(tokens, cotangent, ocean_mask, gain, w_qkv, w_out):
    dim = w_out.shape[0]
    n_lat, n_lon = lax.axis_size(LAT), lax.axis_size(LON)
    place = lax.axis_index(LAT).astype(jnp.int32).reshape(1)
    constant = functools.partial(jnp.asarray, dtype=BF16)
    columns = columns_matrix()
    spread = np.zeros((128, 256), np.float32)
    spread[:, 0:32], spread[:, 128:224] = columns[0:32].T, columns[32:128].T

    def place_of(a, b):
        return a * n_lon + b % n_lon

    south = [(a, a + 1) for a in range(n_lat - 1)]
    diagonal = [(place_of(a, b), place_of(a + 1, b + 1)) for a in range(n_lat - 1) for b in range(n_lon)]
    east = [(b, (b + 1) % n_lon) for b in range(n_lon)]

    def back(pairs):
        return [(target, source) for source, target in pairs]

    lat, diag, lon = call(
        send_kernel, [((192, dim), BF16), ((64, dim), BF16), ((128, dim), BF16)],
        far=(tokens, cotangent, constant(columns)), limit=60,
    )
    lat = lax.ppermute(lat, LAT, back(south))
    diag = lax.ppermute(diag, LAT + LON, back(diagonal))
    lon = lax.ppermute(lon, LON, back(east))
    near = (tokens, constant(constants()), w_qkv, cotangent, w_out)
    near = call(stage_kernel, [(a.shape, BF16) for a in near], far=near)
    half = 6 * dim
    shapes = [(2, half, LANES), (WIN, dim), (96, dim), (96, dim), (160, dim)]
    grads, own_back, lat_back, side_back, edge_back = call(
        window_kernel, [(shape, BF16) for shape in shapes],
        *near, lat, diag, lon, gain,
        scalars=(place, ocean_mask.T),
        scratch=[
            pltpu.VMEM((2, dim, 3 * WIN), BF16),
            pltpu.VMEM((12, 3 * WIN, LANES), BF16),
            pltpu.VMEM((3 * WIN, 3 * dim), BF16),
            pltpu.VMEM((3 * WIN, dim), BF16),
        ],
    )

    side = lax.ppermute(side_back, LON, east)
    mine = (grads[0].astype(F32) + swapped(grads[1]).astype(F32)).astype(BF16)
    mine = summed(exchange(mine.reshape(16, half // 16, LANES), PLANE))
    mine = summed(exchange(mine.reshape(16, half // 256, LANES), RING))
    (rows_back,) = call(
        join_kernel, [((WIN, dim), BF16)], lat_back, side, flops=LONG
    )
    mine, rows_back = tied(mine, rows_back)
    rows_back = lax.ppermute(rows_back, LAT, south)
    mine = spread_along(mine, RING).reshape(half // 16, LANES)
    mine = spread_along(mine, PLANE).reshape(half, LANES)
    (token_grad,) = call(
        token_kernel, [(tokens.shape, BF16)],
        own_back, edge_back, rows_back, side,
        far=(cotangent, constant(spread)), flops=LONG,
    )
    mine, token_grad = tied(mine, token_grad)
    other = swapped(mine)
    qkv_grad, out_grad, gain_grad = call(
        result_kernel, [(w_qkv.shape, BF16), (w_out.shape, BF16), ((dim,), BF16)],
        mine, other, gain,
        scalars=(place,), far=(w_qkv,),
    )
    return token_grad, qkv_grad, out_grad, gain_grad


def solution(mesh):
    fine = Mesh(mesh.devices.reshape(2, 4, 2, 8, 4), ("zhi", "x", "core", "zlo", "y"))
    tiles = P(None, LAT, LON, None)
    return jax.shard_map(
        local,
        mesh=fine,
        in_specs=(tiles, tiles, P(None, LON), P(), P(), P()),
        out_specs=(tiles, P(), P(), P()),
        check_vma=False,
    )
```

```python
import functools

import jax
import jax.numpy as jnp
import numpy as np
from jax import lax
from jax.experimental import pallas as pl
from jax.experimental.pallas import tpu as pltpu
from jax.sharding import Mesh
from jax.sharding import PartitionSpec as P

HEADS = 12
HDIM = 32
PACK = 4
LANES = 128
WIN = 128
LAT = ("zhi", "x", "core")
LON = ("zlo", "y")
PLANE = ("x", "y")
RING = ("zhi", "zlo")
F32 = jnp.float32
BF16 = jnp.bfloat16
LONG = 3 * 10**10


def dot(left, right):
    return jnp.dot(left, right, preferred_element_type=F32)


def dot_nt(left, right):
    return lax.dot_general(left, right, (((1,), (1,)), ((), ())), preferred_element_type=F32)


class Fetch:
    def __init__(self, ref, spot, sem):
        self.spot, self.copy = spot, pltpu.make_async_copy(ref, spot, sem)

    def get(self):
        self.copy.wait()
        return self.spot


def call(kernel, outs, *args, scalars=(), far=(), scratch=(), limit=40, flops=0, spaces=None, after=()):
    n_after = len(after)
    n_scalars, n_far, n_args, n_outs = len(scalars), len(far), len(args), len(outs)

    def body(*refs):
        head, rest = refs[:n_scalars], refs[n_scalars:]
        sources, rest = rest[:n_far], rest[n_far:]
        near, rest = rest[:n_args], rest[n_args + n_after :]
        results, rest = rest[:n_outs], rest[n_outs:]
        if not n_far:
            return kernel(*head, *near, *results, *rest)
        spots, sems, own = rest[:n_far], rest[n_far], rest[n_far + 1 :]
        fetches = [Fetch(sources[i], spots[i], sems.at[i]) for i in range(n_far)]
        for fetch in fetches:
            fetch.copy.start()
        kernel(*head, *fetches, *near, *results, *own)

    specs = [pl.BlockSpec(memory_space=pltpu.SMEM)] * n_scalars
    specs += [pl.BlockSpec(memory_space=pltpu.HBM)] * n_far
    specs += [pl.BlockSpec(memory_space=pltpu.VMEM)] * n_args
    specs += [pl.BlockSpec(memory_space=pl.ANY)] * n_after
    spots = [pltpu.VMEM(a.shape, a.dtype) for a in far]
    if far:
        spots.append(pltpu.SemaphoreType.DMA((n_far,)))
    return pl.pallas_call(
        body,
        out_shape=[jax.ShapeDtypeStruct(s, d) for s, d in outs],
        in_specs=specs,
        out_specs=[pl.BlockSpec(memory_space=space) for space in spaces or [pltpu.VMEM] * n_outs],
        scratch_shapes=spots + list(scratch),
        compiler_params=pltpu.CompilerParams(vmem_limit_bytes=limit * 1024 * 1024),
        name=kernel.__name__,
        cost_estimate=pl.CostEstimate(flops=flops, bytes_accessed=0, transcendentals=0) if flops else None,
    )(*scalars, *far, *args, *after)


PICK = (slice(0, 128), slice(128, 224), slice(256, 288), slice(384, 416))
PUT = 256
EDGE_PICK = (slice(256, 384), slice(384, 416))
EDGE_PUT = 384


def constants():
    pick = np.zeros((2 * WIN, 512), np.float32)
    back = np.zeros((288, 2 * WIN), np.float32)
    edge = np.zeros((WIN, 256), np.float32)
    edge_back = np.zeros((160, WIN), np.float32)
    for w in range(2):
        for level in range(2):
            for r in range(8):
                for c in range(8):
                    col, row, below = 4 + 8 * w + c, r % 4, r // 4
                    token = w * WIN + level * 64 + r * 8 + c
                    corner = level * 16 + row * 4 + col - 16
                    grid = level * 64 + row * 16 + col
                    if col >= 16:
                        pick[token, (256 if below else 384) + corner] = 1
                        back[(224 if below else 256) + corner, token] = 1
                    elif below:
                        inner = level * 48 + row * 12 + col - 4
                        pick[token, 128 + inner] = 1
                        back[128 + inner, token] = 1
                    else:
                        pick[token, grid] = 1
                        back[grid, token] = 1
                    if r < 4:
                        token = w * 64 + level * 32 + r * 8 + c
                        edge[token, 128 + corner if col >= 16 else grid] = 1
                        edge_back[128 + corner if col >= 16 else grid, token] = 1
    packed = np.zeros((544, 512), np.float32)
    packed[0:256] = pick
    packed[256:544, 0:256] = back
    packed[256:384, 256:512] = edge
    packed[384:544, 256:384] = edge_back
    return packed


def columns_matrix():
    columns = np.zeros((128, 128), np.float32)
    for row in range(8):
        for col in range(16):
            at = row * 4 + col if col < 4 else 32 + row * 12 + col - 4
            columns[at, row * 16 + col] = 1
    return columns


def send_kernel(tok, cot, columns, lat_out, diag_out, lon_out):
    refs = [tok.get(), cot.get()]
    pick = columns.get()[...]
    for i, ref in enumerate(refs):
        upper = dot(pick, ref[:, 0:4].reshape(WIN, -1)).astype(BF16)
        lower = dot(pick[0:32], ref[:, 4:8].reshape(WIN, -1)).astype(BF16)
        lat_out[i * 96 : (i + 1) * 96] = upper[32:128]
        diag_out[i * 32 : (i + 1) * 32] = upper[0:32]
        lon_out[i * 32 : (i + 1) * 32] = lower
        lon_out[64 + i * 32 : 64 + (i + 1) * 32] = upper[0:32]


def pause_kernel(place, out):
    out[0] = place[0]


def normalized(x):
    centered = x - jnp.mean(x, -1, keepdims=True)
    rstd = lax.rsqrt(jnp.mean(centered * centered, -1, keepdims=True) + 1e-5)
    return centered * rstd, rstd


def half_sums(left, right, out, half, count):
    dim = left.shape[1]
    for at in range(6):
        j = half * 6 + at
        term = dot(left[j // 9, :, 0:count], right[j, 0:count])
        out[at * dim : (at + 1) * dim] = term.astype(BF16)


def window_kernel(
    place, ocean_mask, tok, const, w_qkv, cot, w_out, lat, diag, lon, gain,
    other, left, right, windows,
    packed, d_att,
):
    dim = lat.shape[1]
    lat_index = place[0]
    core = lax.rem(lat_index, 2)
    last_band = (lat_index == ocean_mask.shape[1] - 1).astype(jnp.int32)
    scale = HDIM ** (-0.5)
    gains = gain[...].reshape(1, dim).astype(F32)
    lane = lax.broadcasted_iota(jnp.int32, (1, LANES), 1)
    masks = [(lane // HDIM == h).astype(F32).astype(BF16) for h in range(PACK)]
    key_at = lax.broadcasted_iota(jnp.int32, (WIN, PACK * WIN), 0)
    query_at = lax.broadcasted_iota(jnp.int32, (WIN, PACK * WIN), 1) % WIN

    def project(x, g, first):
        rows = slice(first, first + x.shape[0])
        windows[rows] = x.astype(BF16)
        normed = normalized(x)[0] * gains
        left[0, :, rows] = normed.T.astype(BF16)
        packed[rows] = dot(normed.astype(BF16), w_qkv[...]).astype(BF16)
        d_att[rows] = dot_nt(g, w_out[...]).astype(BF16)
        for j in range(dim // LANES):
            right[9 + j, rows] = g[:, j * LANES : (j + 1) * LANES]

    def attend(first, differ):
        rows = slice(first, first + WIN)
        for group in range(HEADS // PACK):
            cols = [slice(p * dim + group * LANES, p * dim + (group + 1) * LANES) for p in range(3)]
            query, keys, values = packed[rows, cols[0]], packed[rows, cols[1]], packed[rows, cols[2]]
            d_out = d_att[rows, cols[0]]
            query_heads = jnp.concatenate([query * m for m in masks], 0)
            d_out_heads = jnp.concatenate([d_out * m for m in masks], 0)
            scores = jnp.where(differ, -1e30, dot_nt(keys, query_heads) * scale)
            expo = jnp.exp(scores - jnp.max(scores, 0, keepdims=True))
            probs = expo / jnp.sum(expo, 0, keepdims=True)
            weights = probs.astype(BF16)
            d_probs = dot_nt(values, d_out_heads)
            inner = jnp.sum(d_probs * probs, 0, keepdims=True)
            d_scores = (probs * (d_probs - inner) * scale).astype(BF16)
            values_t = values.T
            keys_t = keys.T
            att_t, d_query_t = [], []
            for h in range(PACK):
                span = slice(h * WIN, (h + 1) * WIN)
                feats = slice(h * HDIM, (h + 1) * HDIM)
                att_t.append(dot(values_t[feats], weights[:, span]))
                d_query_t.append(dot(keys_t[feats], d_scores[:, span]))
            att_rows = slice(group * LANES, (group + 1) * LANES)
            left[1, att_rows, rows] = jnp.concatenate(att_t, 0).astype(BF16)
            right[group, rows] = jnp.concatenate(d_query_t, 0).T.astype(BF16)
            right[3 + group, rows] = dot(d_scores, query_heads).astype(BF16)
            right[6 + group, rows] = dot(weights, d_out_heads).astype(BF16)

    def assembled(i, ref):
        return (
            dot(const[0:256, PICK[0]], ref[:, 4:8].reshape(WIN, dim))
            + dot(const[0:256, PICK[1]], lat[i * 96 : (i + 1) * 96])
            + dot(const[0:256, PICK[2]], diag[i * 32 : (i + 1) * 32])
            + dot(const[0:256, PICK[3]], lon[i * 32 : (i + 1) * 32])
        )

    def ocean(band, rows, size):
        first = lax.broadcasted_iota(jnp.int32, (rows, 1), 0) < size
        return jnp.where(first, ocean_mask[0, band], ocean_mask[1, band]).astype(F32)

    g = (assembled(1, cot) * ocean(lat_index, 2 * WIN, WIN)).astype(BF16)
    project(assembled(0, tok), g, 0)
    lower_differs = ((key_at // 8 % 8 >= 4) != (query_at // 8 % 8 >= 4)).astype(jnp.int32)
    for w in range(2):
        attend(w * WIN, lower_differs * last_band > 0)

    @pl.when(lat_index == 0)
    def _():
        def edge(i, ref):
            return dot(const[256:384, EDGE_PICK[0]], ref[:, 0:4].reshape(WIN, dim)) + dot(
                const[256:384, EDGE_PICK[1]], lon[64 + i * 32 : 64 + (i + 1) * 32]
            )

        last = ocean_mask.shape[1] - 1
        edge_g = (edge(1, cot) * ocean(last, WIN, 64)).astype(BF16)
        project(edge(0, tok), edge_g, 2 * WIN)
        attend(2 * WIN, key_at // 64 != query_at // 64)
        half_sums(left, right, other, 1 - core, 3 * WIN)

    @pl.when(lat_index != 0)
    def _():
        half_sums(left, right, other, 1 - core, 2 * WIN)


def branch_kernel(place, left, right, windows, const, w_qkv, gain, mine, own_back, lat_back, side_back, edge_back):
    dim = windows.shape[1]
    lat_index = place[0]
    core = lax.rem(lat_index, 2)
    gains = gain[...].reshape(1, dim).astype(F32)

    def branch(first, count):
        rows = slice(first, first + count)
        xhat, rstd = normalized(windows[rows].astype(F32))
        d_packed = jnp.concatenate([right[j, rows] for j in range(9)], 1)
        d_normed = dot_nt(d_packed, w_qkv[...])
        d_hat = d_normed * gains
        d_branch = rstd * (
            d_hat
            - jnp.mean(d_hat, -1, keepdims=True)
            - xhat * jnp.mean(d_hat * xhat, -1, keepdims=True)
        )
        return d_branch.astype(BF16)

    @pl.when(lat_index == 0)
    def _():
        half_sums(left, right, mine, core, 3 * WIN)
        edge_back[...] = dot(const[EDGE_PUT : EDGE_PUT + 160, 256:384], branch(2 * WIN, WIN)).astype(BF16)

    @pl.when(lat_index != 0)
    def _():
        half_sums(left, right, mine, core, 2 * WIN)
        edge_back[...] = jnp.zeros_like(edge_back)

    back = dot(const[PUT : PUT + 288, 0:256], branch(0, 2 * WIN)).astype(BF16)
    own_back[...] = back[0:128]
    lat_back[...] = back[128:224]
    side_back[0:64] = back[224:288]
    side_back[64:96] = edge_back[128:160]


def add_kernel(mine, received, out):
    out[...] = (mine[...].astype(F32) + received[...].astype(F32)).astype(BF16)


def join_kernel(lat_back, side, out):
    out[0:96] = lat_back[...]
    out[96:128] = side[0:32]


def token_kernel(cot, spread, own, edge, lat, side, out):
    cot, fill = cot.get(), spread.get()[...]
    lower = own[...].astype(F32) + dot(fill[:, 0:32], side[32:64])
    upper = (
        edge[0:128].astype(F32)
        + dot(fill[:, 0:32], lat[96:128] + side[64:96])
        + dot(fill[:, 128:224], lat[0:96])
    )
    shape = (2, 4) + cot.shape[2:]
    out[:, 0:4] = (cot[:, 0:4].astype(F32) + upper.reshape(shape)).astype(BF16)
    out[:, 4:8] = (cot[:, 4:8].astype(F32) + lower.reshape(shape)).astype(BF16)


def result_kernel(place, w_qkv, mine, other, gain, qkv_out, out_out, gain_out):
    dim = out_out.shape[0]
    w_qkv = w_qkv.get()

    def write(halves):
        along = jnp.zeros((dim, LANES), F32)
        for j in range(12):
            at = (j % 6) * dim
            block = halves[j // 6][at : at + dim]
            if j < 9:
                cols = slice(j * LANES, (j + 1) * LANES)
                qkv_out[:, cols] = block
                along = along + w_qkv[:, cols].astype(F32) * block.astype(F32)
            else:
                out_out[:, (j - 9) * LANES : (j - 8) * LANES] = block
        total = jnp.sum(along.T, 0, keepdims=True)
        gains = gain[...].reshape(1, dim).astype(F32)
        gain_out[...] = (total / gains).astype(BF16).reshape(dim)

    core = lax.rem(place[0], 2)

    @pl.when(core == 0)
    def _():
        write((mine, other))

    @pl.when(core != 0)
    def _():
        write((other, mine))


def exchange(parts, axis):
    return lax.all_to_all(parts, axis, 0, 0, tiled=False)


def summed(parts):
    return jnp.sum(parts.astype(F32), 0).astype(BF16)


def spread_along(part, axis):
    parts = jnp.broadcast_to(part[None], (lax.axis_size(axis),) + part.shape)
    return exchange(parts, axis)


def swapped(array):
    return lax.ppermute(array, "core", [(0, 1), (1, 0)])


def tied(*arrays):
    return lax.optimization_barrier(arrays)


def local(tokens, cotangent, ocean_mask, gain, w_qkv, w_out):
    dim = w_out.shape[0]
    n_lat, n_lon = lax.axis_size(LAT), lax.axis_size(LON)
    place = lax.axis_index(LAT).astype(jnp.int32).reshape(1)
    constant = functools.partial(jnp.asarray, dtype=BF16)
    columns = columns_matrix()
    spread = np.zeros((128, 256), np.float32)
    spread[:, 0:32], spread[:, 128:224] = columns[0:32].T, columns[32:128].T

    def place_of(a, b):
        return a * n_lon + b % n_lon

    south = [(a, a + 1) for a in range(n_lat - 1)]
    diagonal = [(place_of(a, b), place_of(a + 1, b + 1)) for a in range(n_lat - 1) for b in range(n_lon)]
    east = [(b, (b + 1) % n_lon) for b in range(n_lon)]

    def back(pairs):
        return [(target, source) for source, target in pairs]

    lat, diag, lon = call(
        send_kernel, [((192, dim), BF16), ((64, dim), BF16), ((128, dim), BF16)],
        far=(tokens, cotangent, constant(columns)), limit=60,
    )
    lat = lax.ppermute(lat, LAT, back(south))
    diag = lax.ppermute(diag, LAT + LON, back(diagonal))
    lon = lax.ppermute(lon, LON, back(east))
    near = (tokens, constant(constants()), w_qkv, cotangent, w_out)
    (pause,) = call(pause_kernel, [((1,), jnp.int32)], scalars=(place,), limit=8, flops=LONG, spaces=[pltpu.SMEM])
    half = 6 * dim
    shapes = [(half, LANES), (2, dim, 3 * WIN), (12, 3 * WIN, LANES), (3 * WIN, dim)]
    other, left, right, windows = call(
        window_kernel, [(shape, BF16) for shape in shapes],
        *near, lat, diag, lon, gain,
        scalars=(place, ocean_mask.T), after=(pause,),
        scratch=[pltpu.VMEM((3 * WIN, 3 * dim), BF16), pltpu.VMEM((3 * WIN, dim), BF16)],
    )
    shapes = [(half, LANES), (WIN, dim), (96, dim), (96, dim), (160, dim)]
    mine, own_back, lat_back, side_back, edge_back = call(
        branch_kernel, [(shape, BF16) for shape in shapes],
        left, right, windows, near[1], w_qkv, gain,
        scalars=(place,), flops=LONG,
    )

    side = lax.ppermute(side_back, LON, east)
    (mine,) = call(add_kernel, [((half, LANES), BF16)], mine, swapped(other))
    mine = summed(exchange(mine.reshape(16, half // 16, LANES), PLANE))
    mine = summed(exchange(mine.reshape(16, half // 256, LANES), RING))
    (rows_back,) = call(
        join_kernel, [((WIN, dim), BF16)], lat_back, side, flops=LONG
    )
    mine, rows_back = tied(mine, rows_back)
    rows_back = lax.ppermute(rows_back, LAT, south)
    mine = spread_along(mine, RING).reshape(half // 16, LANES)
    mine = spread_along(mine, PLANE).reshape(half, LANES)
    (token_grad,) = call(
        token_kernel, [(tokens.shape, BF16)],
        own_back, edge_back, rows_back, side,
        far=(cotangent, constant(spread)), flops=LONG,
    )
    mine, token_grad = tied(mine, token_grad)
    other = swapped(mine)
    qkv_grad, out_grad, gain_grad = call(
        result_kernel, [(w_qkv.shape, BF16), (w_out.shape, BF16), ((dim,), BF16)],
        mine, other, gain,
        scalars=(place,), far=(w_qkv,),
    )
    return token_grad, qkv_grad, out_grad, gain_grad


def solution(mesh):
    fine = Mesh(mesh.devices.reshape(2, 4, 2, 8, 4), ("zhi", "x", "core", "zlo", "y"))
    tiles = P(None, LAT, LON, None)
    return jax.shard_map(
        local,
        mesh=fine,
        in_specs=(tiles, tiles, P(None, LON), P(), P(), P()),
        out_specs=(tiles, P(), P(), P()),
        check_vma=False,
    )
```

```python
import functools

import jax
import jax.numpy as jnp
import numpy as np
from jax import lax
from jax.experimental import pallas as pl
from jax.experimental.pallas import tpu as pltpu
from jax.sharding import Mesh
from jax.sharding import PartitionSpec as P

HEADS = 12
HDIM = 32
PACK = 4
LANES = 128
WIN = 128
LAT = ("zhi", "x", "core")
LON = ("zlo", "y")
PLANE = ("x", "y")
ALL = ("zhi", "x", "core", "zlo", "y")


def rings(first):
    order = [(first + i) % 16 for i in range(16)]
    return [
        [(((z // 8 * 4 + x) * 2 + core) * 8 + z % 8) * 4 + y for z in order]
        for x in range(4)
        for core in range(2)
        for y in range(4)
    ]


RINGS = rings(8)
F32 = jnp.float32
BF16 = jnp.bfloat16
LONG = 3 * 10**10


def dot(left, right):
    return jnp.dot(left, right, preferred_element_type=F32)


def dot_nt(left, right):
    return lax.dot_general(left, right, (((1,), (1,)), ((), ())), preferred_element_type=F32)


class Fetch:
    def __init__(self, ref, spot, sem):
        self.spot, self.copy = spot, pltpu.make_async_copy(ref, spot, sem)

    def get(self):
        self.copy.wait()
        return self.spot


def call(kernel, outs, *args, scalars=(), far=(), scratch=(), limit=40, flops=0, spaces=None, after=()):
    n_after = len(after)
    n_scalars, n_far, n_args, n_outs = len(scalars), len(far), len(args), len(outs)

    def body(*refs):
        head, rest = refs[:n_scalars], refs[n_scalars:]
        sources, rest = rest[:n_far], rest[n_far:]
        near, rest = rest[:n_args], rest[n_args + n_after :]
        results, rest = rest[:n_outs], rest[n_outs:]
        if not n_far:
            return kernel(*head, *near, *results, *rest)
        spots, sems, own = rest[:n_far], rest[n_far], rest[n_far + 1 :]
        fetches = [Fetch(sources[i], spots[i], sems.at[i]) for i in range(n_far)]
        for fetch in fetches:
            fetch.copy.start()
        kernel(*head, *fetches, *near, *results, *own)

    specs = [pl.BlockSpec(memory_space=pltpu.SMEM)] * n_scalars
    specs += [pl.BlockSpec(memory_space=pltpu.HBM)] * n_far
    specs += [pl.BlockSpec(memory_space=pltpu.VMEM)] * n_args
    specs += [pl.BlockSpec(memory_space=pl.ANY)] * n_after
    spots = [pltpu.VMEM(a.shape, a.dtype) for a in far]
    if far:
        spots.append(pltpu.SemaphoreType.DMA((n_far,)))
    return pl.pallas_call(
        body,
        out_shape=[jax.ShapeDtypeStruct(s, d) for s, d in outs],
        in_specs=specs,
        out_specs=[pl.BlockSpec(memory_space=space) for space in spaces or [pltpu.VMEM] * n_outs],
        scratch_shapes=spots + list(scratch),
        compiler_params=pltpu.CompilerParams(vmem_limit_bytes=limit * 1024 * 1024),
        name=kernel.__name__,
        cost_estimate=pl.CostEstimate(flops=flops, bytes_accessed=0, transcendentals=0) if flops else None,
    )(*scalars, *far, *args, *after)


PICK = slice(0, 288)
PUT = 256
EDGE_PICK = slice(128, 288)
EDGE_PUT = 544


def constants():
    pick = np.zeros((2 * WIN, 288), np.float32)
    back = np.zeros((288, 2 * WIN), np.float32)
    edge = np.zeros((WIN, 160), np.float32)
    edge_back = np.zeros((160, WIN), np.float32)
    for w in range(2):
        for level in range(2):
            for r in range(8):
                for c in range(8):
                    col, row, below = 4 + 8 * w + c, r % 4, r // 4
                    token = w * WIN + level * 64 + r * 8 + c
                    corner = level * 16 + row * 4 + col - 16
                    grid = level * 64 + row * 16 + col
                    if col >= 16:
                        pick[token, (224 if below else 256) + corner] = 1
                        back[(224 if below else 256) + corner, token] = 1
                    elif below:
                        inner = level * 48 + row * 12 + col - 4
                        pick[token, 128 + inner] = 1
                        back[128 + inner, token] = 1
                    else:
                        pick[token, grid] = 1
                        back[grid, token] = 1
                    if r < 4:
                        token = w * 64 + level * 32 + r * 8 + c
                        edge[token, 128 + corner if col >= 16 else grid] = 1
                        edge_back[128 + corner if col >= 16 else grid, token] = 1
    packed = np.zeros((704, 384), np.float32)
    packed[0:256, 0:288] = pick[:, 0:288]
    packed[256:544, 0:256] = back
    packed[544:704, 0:128] = edge_back
    packed[544:672, 128:288] = edge
    return packed


def columns_matrix():
    columns = np.zeros((128, 128), np.float32)
    for row in range(8):
        for col in range(16):
            at = row * 4 + col if col < 4 else 32 + row * 12 + col - 4
            columns[at, row * 16 + col] = 1
    return columns


def send_kernel(tok, cot, columns, lat_out, diag_out, lon_out):
    refs = [tok.get(), cot.get()]
    pick = columns.get()[...]
    for i, ref in enumerate(refs):
        upper = dot(pick, ref[:, 0:4].reshape(WIN, -1)).astype(BF16)
        lower = dot(pick[0:32], ref[:, 4:8].reshape(WIN, -1)).astype(BF16)
        lat_out[i * 96 : (i + 1) * 96] = upper[32:128]
        diag_out[i * 32 : (i + 1) * 32] = upper[0:32]
        lon_out[i * 32 : (i + 1) * 32] = lower
        lon_out[64 + i * 32 : 64 + (i + 1) * 32] = upper[0:32]


def pause_kernel(place, out):
    out[0] = place[0]


def normalized(x):
    centered = x - jnp.mean(x, -1, keepdims=True)
    rstd = lax.rsqrt(jnp.mean(centered * centered, -1, keepdims=True) + 1e-5)
    return centered * rstd, rstd


def half_sums(left, right, out, half, count):
    dim = left.shape[1]
    for at in range(6):
        j = half * 6 + at
        term = dot(left[j // 9, :, 0:count], right[j, 0:count])
        out[at * dim : (at + 1) * dim] = term.astype(BF16)


def window_kernel(
    place, ocean_mask, tok, const, w_qkv, cot, w_out, lat, diag, lon, gain,
    other, left, right, windows,
    packed, d_att,
):
    dim = lat.shape[1]
    lat_index = place[0]
    core = lax.rem(lat_index, 2)
    last_band = (lat_index == ocean_mask.shape[1] - 1).astype(jnp.int32)
    scale = HDIM ** (-0.5)
    gains = gain[...].reshape(1, dim).astype(F32)
    lane = lax.broadcasted_iota(jnp.int32, (1, LANES), 1)
    masks = [(lane // HDIM == h).astype(F32).astype(BF16) for h in range(PACK)]
    key_at = lax.broadcasted_iota(jnp.int32, (WIN, PACK * WIN), 0)
    query_at = lax.broadcasted_iota(jnp.int32, (WIN, PACK * WIN), 1) % WIN

    def project(x, g, first):
        rows = slice(first, first + x.shape[0])
        windows[rows] = x.astype(BF16)
        normed = normalized(x)[0] * gains
        left[0, :, rows] = normed.T.astype(BF16)
        packed[rows] = dot(normed.astype(BF16), w_qkv[...]).astype(BF16)
        d_att[rows] = dot_nt(g, w_out[...]).astype(BF16)
        for j in range(dim // LANES):
            right[9 + j, rows] = g[:, j * LANES : (j + 1) * LANES]

    def attend(first, differ):
        rows = slice(first, first + WIN)
        for group in range(HEADS // PACK):
            cols = [slice(p * dim + group * LANES, p * dim + (group + 1) * LANES) for p in range(3)]
            query, keys, values = packed[rows, cols[0]], packed[rows, cols[1]], packed[rows, cols[2]]
            d_out = d_att[rows, cols[0]]
            query_heads = jnp.concatenate([query * m for m in masks], 0)
            d_out_heads = jnp.concatenate([d_out * m for m in masks], 0)
            scores = jnp.where(differ, -1e30, dot_nt(keys, query_heads) * scale)
            expo = jnp.exp(scores - jnp.max(scores, 0, keepdims=True))
            probs = expo / jnp.sum(expo, 0, keepdims=True)
            weights = probs.astype(BF16)
            d_probs = dot_nt(values, d_out_heads)
            inner = jnp.sum(d_probs * probs, 0, keepdims=True)
            d_scores = (probs * (d_probs - inner) * scale).astype(BF16)
            values_t = values.T
            keys_t = keys.T
            att_t, d_query_t = [], []
            for h in range(PACK):
                span = slice(h * WIN, (h + 1) * WIN)
                feats = slice(h * HDIM, (h + 1) * HDIM)
                att_t.append(dot(values_t[feats], weights[:, span]))
                d_query_t.append(dot(keys_t[feats], d_scores[:, span]))
            att_rows = slice(group * LANES, (group + 1) * LANES)
            left[1, att_rows, rows] = jnp.concatenate(att_t, 0).astype(BF16)
            right[group, rows] = jnp.concatenate(d_query_t, 0).T.astype(BF16)
            right[3 + group, rows] = dot(d_scores, query_heads).astype(BF16)
            right[6 + group, rows] = dot(weights, d_out_heads).astype(BF16)

    def sources(i, ref):
        return jnp.concatenate(
            [
                ref[:, 4:8].reshape(WIN, dim),
                lat[i * 96 : (i + 1) * 96],
                diag[i * 32 : (i + 1) * 32],
                lon[i * 32 : (i + 1) * 32],
            ],
            0,
        )

    def edge_sources(i, ref):
        return jnp.concatenate(
            [ref[:, 0:4].reshape(WIN, dim), lon[64 + i * 32 : 64 + (i + 1) * 32]], 0
        )

    def assembled(matrix, tokens, cotangents):
        both = dot(matrix, jnp.concatenate([tokens, cotangents], 1))
        return both[:, 0:dim], both[:, dim : 2 * dim]

    def ocean(band, rows, size):
        first = lax.broadcasted_iota(jnp.int32, (rows, 1), 0) < size
        return jnp.where(first, ocean_mask[0, band], ocean_mask[1, band]).astype(F32)

    x, g = assembled(const[0:256, PICK], sources(0, tok), sources(1, cot))
    project(x, (g * ocean(lat_index, 2 * WIN, WIN)).astype(BF16), 0)
    lower_differs = ((key_at // 8 % 8 >= 4) != (query_at // 8 % 8 >= 4)).astype(jnp.int32)
    for w in range(2):
        attend(w * WIN, lower_differs * last_band > 0)

    @pl.when(lat_index == 0)
    def _():
        last = ocean_mask.shape[1] - 1
        matrix = const[EDGE_PUT : EDGE_PUT + WIN, EDGE_PICK]
        edge_x, edge_g = assembled(matrix, edge_sources(0, tok), edge_sources(1, cot))
        project(edge_x, (edge_g * ocean(last, WIN, 64)).astype(BF16), 2 * WIN)
        attend(2 * WIN, key_at // 64 != query_at // 64)
        half_sums(left, right, other, 1 - core, 3 * WIN)

    @pl.when(lat_index != 0)
    def _():
        half_sums(left, right, other, 1 - core, 2 * WIN)


def branch_kernel(place, left, right, windows, const, w_qkv, gain, mine, own_back, lat_back, side_back, edge_back):
    dim = windows.shape[1]
    lat_index = place[0]
    core = lax.rem(lat_index, 2)
    gains = gain[...].reshape(1, dim).astype(F32)

    def branch(first, count):
        rows = slice(first, first + count)
        xhat, rstd = normalized(windows[rows].astype(F32))
        d_packed = jnp.concatenate([right[j, rows] for j in range(9)], 1)
        d_normed = dot_nt(d_packed, w_qkv[...])
        d_hat = d_normed * gains
        d_branch = rstd * (
            d_hat
            - jnp.mean(d_hat, -1, keepdims=True)
            - xhat * jnp.mean(d_hat * xhat, -1, keepdims=True)
        )
        return d_branch.astype(BF16)

    @pl.when(lat_index == 0)
    def _():
        half_sums(left, right, mine, core, 3 * WIN)
        edge_back[...] = dot(const[EDGE_PUT : EDGE_PUT + 160, 0:128], branch(2 * WIN, WIN)).astype(BF16)

    @pl.when(lat_index != 0)
    def _():
        half_sums(left, right, mine, core, 2 * WIN)
        edge_back[...] = jnp.zeros_like(edge_back)

    back = dot(const[PUT : PUT + 288, 0:256], branch(0, 2 * WIN)).astype(BF16)
    own_back[...] = back[0:128]
    lat_back[...] = back[128:224]
    side_back[0:64] = back[224:288]
    side_back[64:96] = edge_back[128:160]


def add_kernel(mine, received, out):
    out[...] = (mine[...].astype(F32) + received[...].astype(F32)).astype(BF16)


def join_kernel(lat_back, side, out):
    out[0:96] = lat_back[...]
    out[96:128] = side[0:32]


def token_kernel(cot, spread, own, edge, lat, side, out):
    cot, fill = cot.get(), spread.get()[...]
    lower = own[...].astype(F32) + dot(fill[:, 0:32], side[32:64])
    upper = (
        edge[0:128].astype(F32)
        + dot(fill[:, 0:32], lat[96:128] + side[64:96])
        + dot(fill[:, 128:224], lat[0:96])
    )
    shape = (2, 4) + cot.shape[2:]
    out[:, 0:4] = (cot[:, 0:4].astype(F32) + upper.reshape(shape)).astype(BF16)
    out[:, 4:8] = (cot[:, 4:8].astype(F32) + lower.reshape(shape)).astype(BF16)


def result_kernel(place, w_qkv, mine, other, gain, qkv_out, out_out, gain_out):
    dim = out_out.shape[0]
    w_qkv = w_qkv.get()

    def write(halves):
        along = jnp.zeros((dim, LANES), F32)
        for j in range(12):
            at = (j % 6) * dim
            block = halves[j // 6][at : at + dim]
            if j < 9:
                cols = slice(j * LANES, (j + 1) * LANES)
                qkv_out[:, cols] = block
                along = along + w_qkv[:, cols].astype(F32) * block.astype(F32)
            else:
                out_out[:, (j - 9) * LANES : (j - 8) * LANES] = block
        total = jnp.sum(along.T, 0, keepdims=True)
        gains = gain[...].reshape(1, dim).astype(F32)
        gain_out[...] = (total / gains).astype(BF16).reshape(dim)

    core = lax.rem(place[0], 2)

    @pl.when(core == 0)
    def _():
        write((mine, other))

    @pl.when(core != 0)
    def _():
        write((other, mine))


def exchange(parts, axis):
    return lax.all_to_all(parts, axis, 0, 0, tiled=False)


def summed(parts):
    return jnp.sum(parts.astype(F32), 0).astype(BF16)


def ring_exchange(parts):
    return lax.all_to_all(parts, ALL, 0, 0, axis_index_groups=RINGS, tiled=False)


def copies(part):
    return jnp.broadcast_to(part[None], (16,) + part.shape)


def swapped(array):
    return lax.ppermute(array, "core", [(0, 1), (1, 0)])


def tied(*arrays):
    return lax.optimization_barrier(arrays)


def local(tokens, cotangent, ocean_mask, gain, w_qkv, w_out):
    dim = w_out.shape[0]
    n_lat, n_lon = lax.axis_size(LAT), lax.axis_size(LON)
    place = lax.axis_index(LAT).astype(jnp.int32).reshape(1)
    constant = functools.partial(jnp.asarray, dtype=BF16)
    columns = columns_matrix()
    spread = np.zeros((128, 256), np.float32)
    spread[:, 0:32], spread[:, 128:224] = columns[0:32].T, columns[32:128].T

    def place_of(a, b):
        return a * n_lon + b % n_lon

    south = [(a, a + 1) for a in range(n_lat - 1)]
    diagonal = [(place_of(a, b), place_of(a + 1, b + 1)) for a in range(n_lat - 1) for b in range(n_lon)]
    east = [(b, (b + 1) % n_lon) for b in range(n_lon)]

    def back(pairs):
        return [(target, source) for source, target in pairs]

    lat, diag, lon = call(
        send_kernel, [((192, dim), BF16), ((64, dim), BF16), ((128, dim), BF16)],
        far=(tokens, cotangent, constant(columns)), limit=60,
    )
    lat = lax.ppermute(lat, LAT, back(south))
    diag = lax.ppermute(diag, LAT + LON, back(diagonal))
    lon = lax.ppermute(lon, LON, back(east))
    near = (tokens, constant(constants()), w_qkv, cotangent, w_out)
    (pause,) = call(pause_kernel, [((1,), jnp.int32)], scalars=(place,), limit=8, flops=LONG, spaces=[pltpu.SMEM])
    half = 6 * dim
    shapes = [(half, LANES), (2, dim, 3 * WIN), (12, 3 * WIN, LANES), (3 * WIN, dim)]
    other, left, right, windows = call(
        window_kernel, [(shape, BF16) for shape in shapes],
        *near, lat, diag, lon, gain,
        scalars=(place, ocean_mask.T), after=(pause,),
        scratch=[pltpu.VMEM((3 * WIN, 3 * dim), BF16), pltpu.VMEM((3 * WIN, dim), BF16)],
    )
    shapes = [(half, LANES), (WIN, dim), (96, dim), (96, dim), (160, dim)]
    mine, own_back, lat_back, side_back, edge_back = call(
        branch_kernel, [(shape, BF16) for shape in shapes],
        left, right, windows, near[1], w_qkv, gain,
        scalars=(place,), flops=LONG,
    )

    side = lax.ppermute(side_back, LON, east)
    (mine,) = call(add_kernel, [((half, LANES), BF16)], mine, swapped(other))
    mine = summed(exchange(mine.reshape(16, half // 16, LANES), PLANE))
    mine = summed(ring_exchange(mine.reshape(16, half // 256, LANES)))
    (rows_back,) = call(
        join_kernel, [((WIN, dim), BF16)], lat_back, side, flops=LONG
    )
    mine, rows_back = tied(mine, rows_back)
    rows_back = lax.ppermute(rows_back, LAT, south)
    mine = ring_exchange(copies(mine)).reshape(half // 16, LANES)
    mine = exchange(copies(mine), PLANE).reshape(half, LANES)
    (token_grad,) = call(
        token_kernel, [(tokens.shape, BF16)],
        own_back, edge_back, rows_back, side,
        far=(cotangent, constant(spread)), flops=LONG,
    )
    mine, token_grad = tied(mine, token_grad)
    other = swapped(mine)
    qkv_grad, out_grad, gain_grad = call(
        result_kernel, [(w_qkv.shape, BF16), (w_out.shape, BF16), ((dim,), BF16)],
        mine, other, gain,
        scalars=(place,), far=(w_qkv,),
    )
    return token_grad, qkv_grad, out_grad, gain_grad


def solution(mesh):
    fine = Mesh(mesh.devices.reshape(2, 4, 2, 8, 4), ("zhi", "x", "core", "zlo", "y"))
    tiles = P(None, LAT, LON, None)
    return jax.shard_map(
        local,
        mesh=fine,
        in_specs=(tiles, tiles, P(None, LON), P(), P(), P()),
        out_specs=(tiles, P(), P(), P()),
        check_vma=False,
    )
```

```python
import functools

import jax
import jax.numpy as jnp
import numpy as np
from jax import lax
from jax.experimental import pallas as pl
from jax.experimental.pallas import tpu as pltpu
from jax.sharding import Mesh
from jax.sharding import PartitionSpec as P

HEADS = 12
HDIM = 32
PACK = 4
LANES = 128
WIN = 128
LAT = ("zhi", "x", "core")
LON = ("zlo", "y")
ALL = ("zhi", "x", "core", "zlo", "y")


def rings(first):
    order = [(first + i) % 16 for i in range(16)]
    return [
        [(((z // 8 * 4 + x) * 2 + core) * 8 + z % 8) * 4 + y for z in order]
        for x in range(4)
        for core in range(2)
        for y in range(4)
    ]


RINGS = rings(7)
PLANES = [
    [(((z // 8 * 4 + (x + 3) % 4) * 2 + core) * 8 + z % 8) * 4 + y for x in range(4) for y in range(4)]
    for z in range(16)
    for core in range(2)
]
F32 = jnp.float32
BF16 = jnp.bfloat16
LONG = 3 * 10**10


def dot(left, right):
    return jnp.dot(left, right, preferred_element_type=F32)


def dot_nt(left, right):
    return lax.dot_general(left, right, (((1,), (1,)), ((), ())), preferred_element_type=F32)


class Fetch:
    def __init__(self, ref, spot, sem):
        self.spot, self.copy = spot, pltpu.make_async_copy(ref, spot, sem)

    def get(self):
        self.copy.wait()
        return self.spot


def call(kernel, outs, *args, scalars=(), far=(), scratch=(), limit=40, flops=0, spaces=None, after=()):
    n_after = len(after)
    n_scalars, n_far, n_args, n_outs = len(scalars), len(far), len(args), len(outs)

    def body(*refs):
        head, rest = refs[:n_scalars], refs[n_scalars:]
        sources, rest = rest[:n_far], rest[n_far:]
        near, rest = rest[:n_args], rest[n_args + n_after :]
        results, rest = rest[:n_outs], rest[n_outs:]
        if not n_far:
            return kernel(*head, *near, *results, *rest)
        spots, sems, own = rest[:n_far], rest[n_far], rest[n_far + 1 :]
        fetches = [Fetch(sources[i], spots[i], sems.at[i]) for i in range(n_far)]
        for fetch in fetches:
            fetch.copy.start()
        kernel(*head, *fetches, *near, *results, *own)

    specs = [pl.BlockSpec(memory_space=pltpu.SMEM)] * n_scalars
    specs += [pl.BlockSpec(memory_space=pltpu.HBM)] * n_far
    specs += [pl.BlockSpec(memory_space=pltpu.VMEM)] * n_args
    specs += [pl.BlockSpec(memory_space=pl.ANY)] * n_after
    spots = [pltpu.VMEM(a.shape, a.dtype) for a in far]
    if far:
        spots.append(pltpu.SemaphoreType.DMA((n_far,)))
    return pl.pallas_call(
        body,
        out_shape=[jax.ShapeDtypeStruct(s, d) for s, d in outs],
        in_specs=specs,
        out_specs=[pl.BlockSpec(memory_space=space) for space in spaces or [pltpu.VMEM] * n_outs],
        scratch_shapes=spots + list(scratch),
        compiler_params=pltpu.CompilerParams(vmem_limit_bytes=limit * 1024 * 1024),
        name=kernel.__name__,
        cost_estimate=pl.CostEstimate(flops=flops, bytes_accessed=0, transcendentals=0) if flops else None,
    )(*scalars, *far, *args, *after)


PICK = slice(0, 288)
PUT = 256
EDGE_PICK = slice(128, 288)
EDGE_PUT = 544


def constants():
    pick = np.zeros((2 * WIN, 288), np.float32)
    back = np.zeros((288, 2 * WIN), np.float32)
    edge = np.zeros((WIN, 160), np.float32)
    edge_back = np.zeros((160, WIN), np.float32)
    for w in range(2):
        for level in range(2):
            for r in range(8):
                for c in range(8):
                    col, row, below = 4 + 8 * w + c, r % 4, r // 4
                    token = w * WIN + level * 64 + r * 8 + c
                    corner = level * 16 + row * 4 + col - 16
                    grid = level * 64 + row * 16 + col
                    if col >= 16:
                        pick[token, (224 if below else 256) + corner] = 1
                        back[(224 if below else 256) + corner, token] = 1
                    elif below:
                        inner = level * 48 + row * 12 + col - 4
                        pick[token, 128 + inner] = 1
                        back[128 + inner, token] = 1
                    else:
                        pick[token, grid] = 1
                        back[grid, token] = 1
                    if r < 4:
                        token = w * 64 + level * 32 + r * 8 + c
                        edge[token, 128 + corner if col >= 16 else grid] = 1
                        edge_back[128 + corner if col >= 16 else grid, token] = 1
    packed = np.zeros((704, 384), np.float32)
    packed[0:256, 0:288] = pick[:, 0:288]
    packed[256:544, 0:256] = back
    packed[544:704, 0:128] = edge_back
    packed[544:672, 128:288] = edge
    return packed


def columns_matrix():
    columns = np.zeros((128, 128), np.float32)
    for row in range(8):
        for col in range(16):
            at = row * 4 + col if col < 4 else 32 + row * 12 + col - 4
            columns[at, row * 16 + col] = 1
    return columns


def send_kernel(tok, cot, columns, lat_out, diag_out, lon_out):
    refs = [tok.get(), cot.get()]
    pick = columns.get()[...]
    for i, ref in enumerate(refs):
        upper = dot(pick, ref[:, 0:4].reshape(WIN, -1)).astype(BF16)
        lower = dot(pick[0:32], ref[:, 4:8].reshape(WIN, -1)).astype(BF16)
        lat_out[i * 96 : (i + 1) * 96] = upper[32:128]
        diag_out[i * 32 : (i + 1) * 32] = upper[0:32]
        lon_out[i * 32 : (i + 1) * 32] = lower
        lon_out[64 + i * 32 : 64 + (i + 1) * 32] = upper[0:32]


def pause_kernel(place, out):
    out[0] = place[0]


def normalized(x):
    centered = x - jnp.mean(x, -1, keepdims=True)
    rstd = lax.rsqrt(jnp.mean(centered * centered, -1, keepdims=True) + 1e-5)
    return centered * rstd, rstd


def half_sums(left, right, out, half, count):
    dim = left.shape[1]
    for at in range(6):
        j = half * 6 + at
        term = dot(left[j // 9, :, 0:count], right[j, 0:count])
        out[at * dim : (at + 1) * dim] = term.astype(BF16)


def window_kernel(
    place, ocean_mask, tok, const, w_qkv, cot, w_out, lat, diag, lon, gain,
    other, left, right, windows,
    packed, d_att,
):
    dim = lat.shape[1]
    lat_index = place[0]
    core = lax.rem(lat_index, 2)
    last_band = (lat_index == ocean_mask.shape[1] - 1).astype(jnp.int32)
    scale = HDIM ** (-0.5)
    gains = gain[...].reshape(1, dim).astype(F32)
    lane = lax.broadcasted_iota(jnp.int32, (1, LANES), 1)
    masks = [(lane // HDIM == h).astype(F32).astype(BF16) for h in range(PACK)]
    key_at = lax.broadcasted_iota(jnp.int32, (WIN, PACK * WIN), 0)
    query_at = lax.broadcasted_iota(jnp.int32, (WIN, PACK * WIN), 1) % WIN

    def project(x, g, first):
        rows = slice(first, first + x.shape[0])
        windows[rows] = x.astype(BF16)
        normed = normalized(x)[0] * gains
        left[0, :, rows] = normed.T.astype(BF16)
        packed[rows] = dot(normed.astype(BF16), w_qkv[...]).astype(BF16)
        d_att[rows] = dot_nt(g, w_out[...]).astype(BF16)
        for j in range(dim // LANES):
            right[9 + j, rows] = g[:, j * LANES : (j + 1) * LANES]

    def attend(first, differ):
        rows = slice(first, first + WIN)
        for group in range(HEADS // PACK):
            cols = [slice(p * dim + group * LANES, p * dim + (group + 1) * LANES) for p in range(3)]
            query, keys, values = packed[rows, cols[0]], packed[rows, cols[1]], packed[rows, cols[2]]
            d_out = d_att[rows, cols[0]]
            query_heads = jnp.concatenate([query * m for m in masks], 0)
            d_out_heads = jnp.concatenate([d_out * m for m in masks], 0)
            scores = jnp.where(differ, -1e30, dot_nt(keys, query_heads) * scale)
            expo = jnp.exp(scores - jnp.max(scores, 0, keepdims=True))
            probs = expo / jnp.sum(expo, 0, keepdims=True)
            weights = probs.astype(BF16)
            d_probs = dot_nt(values, d_out_heads)
            inner = jnp.sum(d_probs * probs, 0, keepdims=True)
            d_scores = (probs * (d_probs - inner) * scale).astype(BF16)
            values_t = values.T
            keys_t = keys.T
            att_t, d_query_t = [], []
            for h in range(PACK):
                span = slice(h * WIN, (h + 1) * WIN)
                feats = slice(h * HDIM, (h + 1) * HDIM)
                att_t.append(dot(values_t[feats], weights[:, span]))
                d_query_t.append(dot(keys_t[feats], d_scores[:, span]))
            att_rows = slice(group * LANES, (group + 1) * LANES)
            left[1, att_rows, rows] = jnp.concatenate(att_t, 0).astype(BF16)
            right[group, rows] = jnp.concatenate(d_query_t, 0).T.astype(BF16)
            right[3 + group, rows] = dot(d_scores, query_heads).astype(BF16)
            right[6 + group, rows] = dot(weights, d_out_heads).astype(BF16)

    def sources(i, ref):
        return jnp.concatenate(
            [
                ref[:, 4:8].reshape(WIN, dim),
                lat[i * 96 : (i + 1) * 96],
                diag[i * 32 : (i + 1) * 32],
                lon[i * 32 : (i + 1) * 32],
            ],
            0,
        )

    def edge_sources(i, ref):
        return jnp.concatenate(
            [ref[:, 0:4].reshape(WIN, dim), lon[64 + i * 32 : 64 + (i + 1) * 32]], 0
        )

    def assembled(matrix, tokens, cotangents):
        both = dot(matrix, jnp.concatenate([tokens, cotangents], 1))
        return both[:, 0:dim], both[:, dim : 2 * dim]

    def ocean(band, rows, size):
        first = lax.broadcasted_iota(jnp.int32, (rows, 1), 0) < size
        return jnp.where(first, ocean_mask[0, band], ocean_mask[1, band]).astype(F32)

    x, g = assembled(const[0:256, PICK], sources(0, tok), sources(1, cot))
    project(x, (g * ocean(lat_index, 2 * WIN, WIN)).astype(BF16), 0)
    lower_differs = ((key_at // 8 % 8 >= 4) != (query_at // 8 % 8 >= 4)).astype(jnp.int32)
    for w in range(2):
        attend(w * WIN, lower_differs * last_band > 0)

    @pl.when(lat_index == 0)
    def _():
        last = ocean_mask.shape[1] - 1
        matrix = const[EDGE_PUT : EDGE_PUT + WIN, EDGE_PICK]
        edge_x, edge_g = assembled(matrix, edge_sources(0, tok), edge_sources(1, cot))
        project(edge_x, (edge_g * ocean(last, WIN, 64)).astype(BF16), 2 * WIN)
        attend(2 * WIN, key_at // 64 != query_at // 64)
        half_sums(left, right, other, 1 - core, 3 * WIN)

    @pl.when(lat_index != 0)
    def _():
        half_sums(left, right, other, 1 - core, 2 * WIN)


def branch_kernel(place, left, right, windows, const, w_qkv, gain, mine, own_back, lat_back, side_back, edge_back):
    dim = windows.shape[1]
    lat_index = place[0]
    core = lax.rem(lat_index, 2)
    gains = gain[...].reshape(1, dim).astype(F32)

    def branch(first, count):
        rows = slice(first, first + count)
        xhat, rstd = normalized(windows[rows].astype(F32))
        d_packed = jnp.concatenate([right[j, rows] for j in range(9)], 1)
        d_normed = dot_nt(d_packed, w_qkv[...])
        d_hat = d_normed * gains
        d_branch = rstd * (
            d_hat
            - jnp.mean(d_hat, -1, keepdims=True)
            - xhat * jnp.mean(d_hat * xhat, -1, keepdims=True)
        )
        return d_branch.astype(BF16)

    @pl.when(lat_index == 0)
    def _():
        half_sums(left, right, mine, core, 3 * WIN)
        edge_back[...] = dot(const[EDGE_PUT : EDGE_PUT + 160, 0:128], branch(2 * WIN, WIN)).astype(BF16)

    @pl.when(lat_index != 0)
    def _():
        half_sums(left, right, mine, core, 2 * WIN)
        edge_back[...] = jnp.zeros_like(edge_back)

    back = dot(const[PUT : PUT + 288, 0:256], branch(0, 2 * WIN)).astype(BF16)
    own_back[...] = back[0:128]
    lat_back[...] = back[128:224]
    side_back[0:64] = back[224:288]
    side_back[64:96] = edge_back[128:160]


def add_kernel(mine, received, out):
    out[...] = (mine[...].astype(F32) + received[...].astype(F32)).astype(BF16)


def join_kernel(lat_back, side, out):
    out[0:96] = lat_back[...]
    out[96:128] = side[0:32]


def token_kernel(cot, spread, own, edge, lat, side, out):
    cot, fill = cot.get(), spread.get()[...]
    lower = own[...].astype(F32) + dot(fill[:, 0:32], side[32:64])
    upper = (
        edge[0:128].astype(F32)
        + dot(fill[:, 0:32], lat[96:128] + side[64:96])
        + dot(fill[:, 128:224], lat[0:96])
    )
    shape = (2, 4) + cot.shape[2:]
    out[:, 0:4] = (cot[:, 0:4].astype(F32) + upper.reshape(shape)).astype(BF16)
    out[:, 4:8] = (cot[:, 4:8].astype(F32) + lower.reshape(shape)).astype(BF16)


def result_kernel(place, w_qkv, mine, other, gain, qkv_out, out_out, gain_out):
    dim = out_out.shape[0]
    w_qkv = w_qkv.get()

    def write(halves):
        along = jnp.zeros((dim, LANES), F32)
        for j in range(12):
            at = (j % 6) * dim
            block = halves[j // 6][at : at + dim]
            if j < 9:
                cols = slice(j * LANES, (j + 1) * LANES)
                qkv_out[:, cols] = block
                along = along + w_qkv[:, cols].astype(F32) * block.astype(F32)
            else:
                out_out[:, (j - 9) * LANES : (j - 8) * LANES] = block
        total = jnp.sum(along.T, 0, keepdims=True)
        gains = gain[...].reshape(1, dim).astype(F32)
        gain_out[...] = (total / gains).astype(BF16).reshape(dim)

    core = lax.rem(place[0], 2)

    @pl.when(core == 0)
    def _():
        write((mine, other))

    @pl.when(core != 0)
    def _():
        write((other, mine))


def exchange(parts, groups):
    return lax.all_to_all(parts, ALL, 0, 0, axis_index_groups=groups, tiled=False)


def summed(parts):
    return jnp.sum(parts.astype(F32), 0).astype(BF16)


def copies(part):
    return jnp.broadcast_to(part[None], (16,) + part.shape)


def swapped(array):
    return lax.ppermute(array, "core", [(0, 1), (1, 0)])


def tied(*arrays):
    return lax.optimization_barrier(arrays)


def local(tokens, cotangent, ocean_mask, gain, w_qkv, w_out):
    dim = w_out.shape[0]
    n_lat, n_lon = lax.axis_size(LAT), lax.axis_size(LON)
    place = lax.axis_index(LAT).astype(jnp.int32).reshape(1)
    constant = functools.partial(jnp.asarray, dtype=BF16)
    columns = columns_matrix()
    spread = np.zeros((128, 256), np.float32)
    spread[:, 0:32], spread[:, 128:224] = columns[0:32].T, columns[32:128].T

    def place_of(a, b):
        return a * n_lon + b % n_lon

    south = [(a, a + 1) for a in range(n_lat - 1)]
    diagonal = [(place_of(a, b), place_of(a + 1, b + 1)) for a in range(n_lat - 1) for b in range(n_lon)]
    east = [(b, (b + 1) % n_lon) for b in range(n_lon)]

    def back(pairs):
        return [(target, source) for source, target in pairs]

    lat, diag, lon = call(
        send_kernel, [((192, dim), BF16), ((64, dim), BF16), ((128, dim), BF16)],
        far=(tokens, cotangent, constant(columns)), limit=60,
    )
    lat = lax.ppermute(lat, LAT, back(south))
    diag = lax.ppermute(diag, LAT + LON, back(diagonal))
    lon = lax.ppermute(lon, LON, back(east))
    near = (tokens, constant(constants()), w_qkv, cotangent, w_out)
    (pause,) = call(pause_kernel, [((1,), jnp.int32)], scalars=(place,), limit=8, flops=LONG, spaces=[pltpu.SMEM])
    half = 6 * dim
    shapes = [(half, LANES), (2, dim, 3 * WIN), (12, 3 * WIN, LANES), (3 * WIN, dim)]
    other, left, right, windows = call(
        window_kernel, [(shape, BF16) for shape in shapes],
        *near, lat, diag, lon, gain,
        scalars=(place, ocean_mask.T), after=(pause,),
        scratch=[pltpu.VMEM((3 * WIN, 3 * dim), BF16), pltpu.VMEM((3 * WIN, dim), BF16)],
    )
    shapes = [(half, LANES), (WIN, dim), (96, dim), (96, dim), (160, dim)]
    mine, own_back, lat_back, side_back, edge_back = call(
        branch_kernel, [(shape, BF16) for shape in shapes],
        left, right, windows, near[1], w_qkv, gain,
        scalars=(place,), flops=LONG,
    )

    side = lax.ppermute(side_back, LON, east)
    (mine,) = call(add_kernel, [((half, LANES), BF16)], mine, swapped(other))
    mine = summed(exchange(mine.reshape(16, half // 16, LANES), PLANES))
    mine = summed(exchange(mine.reshape(16, half // 256, LANES), RINGS))
    (rows_back,) = call(
        join_kernel, [((WIN, dim), BF16)], lat_back, side, flops=LONG
    )
    mine, rows_back = tied(mine, rows_back)
    rows_back = lax.ppermute(rows_back, LAT, south)
    mine = exchange(copies(mine), RINGS).reshape(half // 16, LANES)
    mine = exchange(copies(mine), PLANES).reshape(half, LANES)
    (token_grad,) = call(
        token_kernel, [(tokens.shape, BF16)],
        own_back, edge_back, rows_back, side,
        far=(cotangent, constant(spread)), flops=LONG,
    )
    mine, token_grad = tied(mine, token_grad)
    other = swapped(mine)
    qkv_grad, out_grad, gain_grad = call(
        result_kernel, [(w_qkv.shape, BF16), (w_out.shape, BF16), ((dim,), BF16)],
        mine, other, gain,
        scalars=(place,), far=(w_qkv,),
    )
    return token_grad, qkv_grad, out_grad, gain_grad


def solution(mesh):
    fine = Mesh(mesh.devices.reshape(2, 4, 2, 8, 4), ("zhi", "x", "core", "zlo", "y"))
    tiles = P(None, LAT, LON, None)
    return jax.shard_map(
        local,
        mesh=fine,
        in_specs=(tiles, tiles, P(None, LON), P(), P(), P()),
        out_specs=(tiles, P(), P(), P()),
        check_vma=False,
    )
```

```python
import functools

import jax
import jax.numpy as jnp
import numpy as np
from jax import lax
from jax.experimental import pallas as pl
from jax.experimental.pallas import tpu as pltpu
from jax.sharding import Mesh
from jax.sharding import PartitionSpec as P

HEADS = 12
HDIM = 32
PACK = 4
LANES = 128
WIN = 128
LAT = ("zhi", "x", "core")
LON = ("zlo", "y")
ALL = ("zhi", "x", "core", "zlo", "y")


def rings(first):
    order = [(first + i) % 16 for i in range(16)]
    return [
        [(((z // 8 * 4 + x) * 2 + core) * 8 + z % 8) * 4 + y for z in order]
        for x in range(4)
        for core in range(2)
        for y in range(4)
    ]


RINGS = rings(7)
PLANES = [
    [(((z // 8 * 4 + (x + 3) % 4) * 2 + core) * 8 + z % 8) * 4 + y for x in range(4) for y in range(4)]
    for z in range(16)
    for core in range(2)
]
F32 = jnp.float32
BF16 = jnp.bfloat16
LONG = 3 * 10**10


def dot(left, right):
    return jnp.dot(left, right, preferred_element_type=F32)


def dot_nt(left, right):
    return lax.dot_general(left, right, (((1,), (1,)), ((), ())), preferred_element_type=F32)


class Fetch:
    def __init__(self, ref, spot, sem):
        self.spot, self.copy = spot, pltpu.make_async_copy(ref, spot, sem)

    def get(self):
        self.copy.wait()
        return self.spot


def call(kernel, outs, *args, scalars=(), far=(), scratch=(), limit=40, flops=0, spaces=None, after=()):
    n_after = len(after)
    n_scalars, n_far, n_args, n_outs = len(scalars), len(far), len(args), len(outs)

    def body(*refs):
        head, rest = refs[:n_scalars], refs[n_scalars:]
        sources, rest = rest[:n_far], rest[n_far:]
        near, rest = rest[:n_args], rest[n_args + n_after :]
        results, rest = rest[:n_outs], rest[n_outs:]
        if not n_far:
            return kernel(*head, *near, *results, *rest)
        spots, sems, own = rest[:n_far], rest[n_far], rest[n_far + 1 :]
        fetches = [Fetch(sources[i], spots[i], sems.at[i]) for i in range(n_far)]
        for fetch in fetches:
            fetch.copy.start()
        kernel(*head, *fetches, *near, *results, *own)

    specs = [pl.BlockSpec(memory_space=pltpu.SMEM)] * n_scalars
    specs += [pl.BlockSpec(memory_space=pltpu.HBM)] * n_far
    specs += [pl.BlockSpec(memory_space=pltpu.VMEM)] * n_args
    specs += [pl.BlockSpec(memory_space=pl.ANY)] * n_after
    spots = [pltpu.VMEM(a.shape, a.dtype) for a in far]
    if far:
        spots.append(pltpu.SemaphoreType.DMA((n_far,)))
    return pl.pallas_call(
        body,
        out_shape=[jax.ShapeDtypeStruct(s, d) for s, d in outs],
        in_specs=specs,
        out_specs=[pl.BlockSpec(memory_space=space) for space in spaces or [pltpu.VMEM] * n_outs],
        scratch_shapes=spots + list(scratch),
        compiler_params=pltpu.CompilerParams(vmem_limit_bytes=limit * 1024 * 1024),
        name=kernel.__name__,
        cost_estimate=pl.CostEstimate(flops=flops, bytes_accessed=0, transcendentals=0) if flops else None,
    )(*scalars, *far, *args, *after)


PICK = slice(0, 288)
PUT = 256
EDGE_PICK = slice(128, 288)
EDGE_PUT = 544


def constants():
    pick = np.zeros((2 * WIN, 288), np.float32)
    back = np.zeros((288, 2 * WIN), np.float32)
    edge = np.zeros((WIN, 160), np.float32)
    edge_back = np.zeros((160, WIN), np.float32)
    for w in range(2):
        for level in range(2):
            for r in range(8):
                for c in range(8):
                    col, row, below = 4 + 8 * w + c, r % 4, r // 4
                    token = w * WIN + level * 64 + r * 8 + c
                    corner = level * 16 + row * 4 + col - 16
                    grid = level * 64 + row * 16 + col
                    if col >= 16:
                        pick[token, (224 if below else 256) + corner] = 1
                        back[(224 if below else 256) + corner, token] = 1
                    elif below:
                        inner = level * 48 + row * 12 + col - 4
                        pick[token, 128 + inner] = 1
                        back[128 + inner, token] = 1
                    else:
                        pick[token, grid] = 1
                        back[grid, token] = 1
                    if r < 4:
                        token = w * 64 + level * 32 + r * 8 + c
                        edge[token, 128 + corner if col >= 16 else grid] = 1
                        edge_back[128 + corner if col >= 16 else grid, token] = 1
    packed = np.zeros((704, 384), np.float32)
    packed[0:256, 0:288] = pick[:, 0:288]
    packed[256:544, 0:256] = back
    packed[544:704, 0:128] = edge_back
    packed[544:672, 128:288] = edge
    return packed


def columns_matrix():
    columns = np.zeros((128, 128), np.float32)
    for row in range(8):
        for col in range(16):
            at = row * 4 + col if col < 4 else 32 + row * 12 + col - 4
            columns[at, row * 16 + col] = 1
    return columns


def send_kernel(tok, cot, columns, lat_out, diag_out, lon_out):
    pick = columns.get()[...]
    for i, fetch in enumerate((tok, cot)):
        ref = fetch.get()
        upper = dot(pick, ref[:, 0:4].reshape(WIN, -1)).astype(BF16)
        lower = dot(pick[0:32], ref[:, 4:8].reshape(WIN, -1)).astype(BF16)
        lat_out[i * 96 : (i + 1) * 96] = upper[32:128]
        diag_out[i * 32 : (i + 1) * 32] = upper[0:32]
        lon_out[i * 32 : (i + 1) * 32] = lower
        lon_out[64 + i * 32 : 64 + (i + 1) * 32] = upper[0:32]


def pause_kernel(place, out):
    out[0] = place[0]


def normalized(x):
    centered = x - jnp.mean(x, -1, keepdims=True)
    rstd = lax.rsqrt(jnp.mean(centered * centered, -1, keepdims=True) + 1e-5)
    return centered * rstd, rstd


def half_sums(left, right, out, half, count):
    dim = left.shape[1]
    for at in range(6):
        j = half * 6 + at
        term = dot(left[j // 9, :, 0:count], right[j, 0:count])
        out[at * dim : (at + 1) * dim] = term.astype(BF16)


def window_kernel(
    place, ocean_mask, tok, const, w_qkv, cot, w_out, lat, diag, lon, gain,
    other, left, right, windows,
    packed, d_att,
):
    dim = lat.shape[1]
    lat_index = place[0]
    core = lax.rem(lat_index, 2)
    last_band = (lat_index == ocean_mask.shape[1] - 1).astype(jnp.int32)
    scale = HDIM ** (-0.5)
    gains = gain[...].reshape(1, dim).astype(F32)
    lane = lax.broadcasted_iota(jnp.int32, (1, LANES), 1)
    masks = [(lane // HDIM == h).astype(F32).astype(BF16) for h in range(PACK)]
    key_at = lax.broadcasted_iota(jnp.int32, (WIN, PACK * WIN), 0)
    query_at = lax.broadcasted_iota(jnp.int32, (WIN, PACK * WIN), 1) % WIN

    def project(x, g, first):
        rows = slice(first, first + x.shape[0])
        windows[rows] = x.astype(BF16)
        normed = normalized(x)[0] * gains
        left[0, :, rows] = normed.T.astype(BF16)
        packed[rows] = dot(normed.astype(BF16), w_qkv[...]).astype(BF16)
        d_att[rows] = dot_nt(g, w_out[...]).astype(BF16)
        for j in range(dim // LANES):
            right[9 + j, rows] = g[:, j * LANES : (j + 1) * LANES]

    def attend(first, differ):
        rows = slice(first, first + WIN)
        for group in range(HEADS // PACK):
            cols = [slice(p * dim + group * LANES, p * dim + (group + 1) * LANES) for p in range(3)]
            query, keys, values = packed[rows, cols[0]], packed[rows, cols[1]], packed[rows, cols[2]]
            d_out = d_att[rows, cols[0]]
            query_heads = jnp.concatenate([query * m for m in masks], 0)
            d_out_heads = jnp.concatenate([d_out * m for m in masks], 0)
            scores = jnp.where(differ, -1e30, dot_nt(keys, query_heads) * scale)
            expo = jnp.exp(scores - jnp.max(scores, 0, keepdims=True))
            probs = expo / jnp.sum(expo, 0, keepdims=True)
            weights = probs.astype(BF16)
            d_probs = dot_nt(values, d_out_heads)
            inner = jnp.sum(d_probs * probs, 0, keepdims=True)
            d_scores = (probs * (d_probs - inner) * scale).astype(BF16)
            values_t = values.T
            keys_t = keys.T
            att_t, d_query_t = [], []
            for h in range(PACK):
                span = slice(h * WIN, (h + 1) * WIN)
                feats = slice(h * HDIM, (h + 1) * HDIM)
                att_t.append(dot(values_t[feats], weights[:, span]))
                d_query_t.append(dot(keys_t[feats], d_scores[:, span]))
            att_rows = slice(group * LANES, (group + 1) * LANES)
            left[1, att_rows, rows] = jnp.concatenate(att_t, 0).astype(BF16)
            right[group, rows] = jnp.concatenate(d_query_t, 0).T.astype(BF16)
            right[3 + group, rows] = dot(d_scores, query_heads).astype(BF16)
            right[6 + group, rows] = dot(weights, d_out_heads).astype(BF16)

    def sources(i, ref):
        return jnp.concatenate(
            [
                ref[:, 4:8].reshape(WIN, dim),
                lat[i * 96 : (i + 1) * 96],
                diag[i * 32 : (i + 1) * 32],
                lon[i * 32 : (i + 1) * 32],
            ],
            0,
        )

    def edge_sources(i, ref):
        return jnp.concatenate(
            [ref[:, 0:4].reshape(WIN, dim), lon[64 + i * 32 : 64 + (i + 1) * 32]], 0
        )

    def assembled(matrix, tokens, cotangents):
        both = dot(matrix, jnp.concatenate([tokens, cotangents], 1))
        return both[:, 0:dim], both[:, dim : 2 * dim]

    def ocean(band, rows, size):
        first = lax.broadcasted_iota(jnp.int32, (rows, 1), 0) < size
        return jnp.where(first, ocean_mask[0, band], ocean_mask[1, band]).astype(F32)

    x, g = assembled(const[0:256, PICK], sources(0, tok), sources(1, cot))
    project(x, (g * ocean(lat_index, 2 * WIN, WIN)).astype(BF16), 0)
    lower_differs = ((key_at // 8 % 8 >= 4) != (query_at // 8 % 8 >= 4)).astype(jnp.int32)
    for w in range(2):
        attend(w * WIN, lower_differs * last_band > 0)

    @pl.when(lat_index == 0)
    def _():
        last = ocean_mask.shape[1] - 1
        matrix = const[EDGE_PUT : EDGE_PUT + WIN, EDGE_PICK]
        edge_x, edge_g = assembled(matrix, edge_sources(0, tok), edge_sources(1, cot))
        project(edge_x, (edge_g * ocean(last, WIN, 64)).astype(BF16), 2 * WIN)
        attend(2 * WIN, key_at // 64 != query_at // 64)
        half_sums(left, right, other, 1 - core, 3 * WIN)

    @pl.when(lat_index != 0)
    def _():
        half_sums(left, right, other, 1 - core, 2 * WIN)


def branch_kernel(place, left, right, windows, const, w_qkv, gain, mine, own_back, lat_back, side_back, edge_back):
    dim = windows.shape[1]
    lat_index = place[0]
    core = lax.rem(lat_index, 2)
    gains = gain[...].reshape(1, dim).astype(F32)

    def branch(first, count):
        rows = slice(first, first + count)
        xhat, rstd = normalized(windows[rows].astype(F32))
        d_packed = jnp.concatenate([right[j, rows] for j in range(9)], 1)
        d_normed = dot_nt(d_packed, w_qkv[...])
        d_hat = d_normed * gains
        d_branch = rstd * (
            d_hat
            - jnp.mean(d_hat, -1, keepdims=True)
            - xhat * jnp.mean(d_hat * xhat, -1, keepdims=True)
        )
        return d_branch.astype(BF16)

    @pl.when(lat_index == 0)
    def _():
        half_sums(left, right, mine, core, 3 * WIN)
        edge_back[...] = dot(const[EDGE_PUT : EDGE_PUT + 160, 0:128], branch(2 * WIN, WIN)).astype(BF16)

    @pl.when(lat_index != 0)
    def _():
        half_sums(left, right, mine, core, 2 * WIN)
        edge_back[...] = jnp.zeros_like(edge_back)

    back = dot(const[PUT : PUT + 288, 0:256], branch(0, 2 * WIN)).astype(BF16)
    own_back[...] = back[0:128]
    lat_back[...] = back[128:224]
    side_back[0:64] = back[224:288]
    side_back[64:96] = edge_back[128:160]


def add_kernel(mine, received, out):
    out[...] = (mine[...].astype(F32) + received[...].astype(F32)).astype(BF16)


def join_kernel(lat_back, side, out):
    out[0:96] = lat_back[...]
    out[96:128] = side[0:32]


def token_kernel(cot, spread, own, edge, lat, side, out):
    cot, fill = cot.get(), spread.get()[...]
    lower = own[...].astype(F32) + dot(fill[:, 0:32], side[32:64])
    upper = (
        edge[0:128].astype(F32)
        + dot(fill[:, 0:32], lat[96:128] + side[64:96])
        + dot(fill[:, 128:224], lat[0:96])
    )
    shape = (2, 4) + cot.shape[2:]
    out[:, 0:4] = (cot[:, 0:4].astype(F32) + upper.reshape(shape)).astype(BF16)
    out[:, 4:8] = (cot[:, 4:8].astype(F32) + lower.reshape(shape)).astype(BF16)


def result_kernel(place, w_qkv, mine, other, gain, qkv_out, out_out, gain_out):
    dim = out_out.shape[0]
    w_qkv = w_qkv.get()

    def write(halves):
        along = jnp.zeros((dim, LANES), F32)
        for j in range(12):
            at = (j % 6) * dim
            block = halves[j // 6][at : at + dim]
            if j < 9:
                cols = slice(j * LANES, (j + 1) * LANES)
                qkv_out[:, cols] = block
                along = along + w_qkv[:, cols].astype(F32) * block.astype(F32)
            else:
                out_out[:, (j - 9) * LANES : (j - 8) * LANES] = block
        total = jnp.sum(along.T, 0, keepdims=True)
        gains = gain[...].reshape(1, dim).astype(F32)
        gain_out[...] = (total / gains).astype(BF16).reshape(dim)

    core = lax.rem(place[0], 2)

    @pl.when(core == 0)
    def _():
        write((mine, other))

    @pl.when(core != 0)
    def _():
        write((other, mine))


def exchange(parts, groups):
    return lax.all_to_all(parts, ALL, 0, 0, axis_index_groups=groups, tiled=False)


def summed(parts):
    return jnp.sum(parts.astype(F32), 0).astype(BF16)


def copies(part):
    return jnp.broadcast_to(part[None], (16,) + part.shape)


def swapped(array):
    return lax.ppermute(array, "core", [(0, 1), (1, 0)])


def tied(*arrays):
    return lax.optimization_barrier(arrays)


def local(tokens, cotangent, ocean_mask, gain, w_qkv, w_out):
    dim = w_out.shape[0]
    n_lat, n_lon = lax.axis_size(LAT), lax.axis_size(LON)
    place = lax.axis_index(LAT).astype(jnp.int32).reshape(1)
    constant = functools.partial(jnp.asarray, dtype=BF16)
    columns = columns_matrix()
    spread = np.zeros((128, 256), np.float32)
    spread[:, 0:32], spread[:, 128:224] = columns[0:32].T, columns[32:128].T

    def place_of(a, b):
        return a * n_lon + b % n_lon

    south = [(a, a + 1) for a in range(n_lat - 1)]
    diagonal = [(place_of(a, b), place_of(a + 1, b + 1)) for a in range(n_lat - 1) for b in range(n_lon)]
    east = [(b, (b + 1) % n_lon) for b in range(n_lon)]

    def back(pairs):
        return [(target, source) for source, target in pairs]

    lat, diag, lon = call(
        send_kernel, [((192, dim), BF16), ((64, dim), BF16), ((128, dim), BF16)],
        far=(tokens, cotangent, constant(columns)), limit=60,
    )
    lat = lax.ppermute(lat, LAT, back(south))
    diag = lax.ppermute(diag, LAT + LON, back(diagonal))
    lon = lax.ppermute(lon, LON, back(east))
    near = (tokens, constant(constants()), w_qkv, cotangent, w_out)
    (pause,) = call(pause_kernel, [((1,), jnp.int32)], scalars=(place,), limit=8, flops=LONG, spaces=[pltpu.SMEM])
    half = 6 * dim
    shapes = [(half, LANES), (2, dim, 3 * WIN), (12, 3 * WIN, LANES), (3 * WIN, dim)]
    other, left, right, windows = call(
        window_kernel, [(shape, BF16) for shape in shapes],
        *near, lat, diag, lon, gain,
        scalars=(place, ocean_mask.T), after=(pause,),
        scratch=[pltpu.VMEM((3 * WIN, 3 * dim), BF16), pltpu.VMEM((3 * WIN, dim), BF16)],
    )
    shapes = [(half, LANES), (WIN, dim), (96, dim), (96, dim), (160, dim)]
    mine, own_back, lat_back, side_back, edge_back = call(
        branch_kernel, [(shape, BF16) for shape in shapes],
        left, right, windows, near[1], w_qkv, gain,
        scalars=(place,), flops=LONG,
    )

    side = lax.ppermute(side_back, LON, east)
    (mine,) = call(add_kernel, [((half, LANES), BF16)], mine, swapped(other))
    mine = summed(exchange(mine.reshape(16, half // 16, LANES), PLANES))
    mine = summed(exchange(mine.reshape(16, half // 256, LANES), RINGS))
    (rows_back,) = call(
        join_kernel, [((WIN, dim), BF16)], lat_back, side, flops=LONG
    )
    mine, rows_back = tied(mine, rows_back)
    rows_back = lax.ppermute(rows_back, LAT, south)
    mine = exchange(copies(mine), RINGS).reshape(half // 16, LANES)
    mine = exchange(copies(mine), PLANES).reshape(half, LANES)
    (token_grad,) = call(
        token_kernel, [(tokens.shape, BF16)],
        own_back, edge_back, rows_back, side,
        far=(cotangent, constant(spread)), flops=LONG,
    )
    mine, token_grad = tied(mine, token_grad)
    other = swapped(mine)
    qkv_grad, out_grad, gain_grad = call(
        result_kernel, [(w_qkv.shape, BF16), (w_out.shape, BF16), ((dim,), BF16)],
        mine, other, gain,
        scalars=(place,), far=(w_qkv,),
    )
    return token_grad, qkv_grad, out_grad, gain_grad


def solution(mesh):
    fine = Mesh(mesh.devices.reshape(2, 4, 2, 8, 4), ("zhi", "x", "core", "zlo", "y"))
    tiles = P(None, LAT, LON, None)
    return jax.shard_map(
        local,
        mesh=fine,
        in_specs=(tiles, tiles, P(None, LON), P(), P(), P()),
        out_specs=(tiles, P(), P(), P()),
        check_vma=False,
    )
```

```python
import functools

import jax
import jax.numpy as jnp
import numpy as np
from jax import lax
from jax.experimental import pallas as pl
from jax.experimental.pallas import tpu as pltpu
from jax.sharding import Mesh
from jax.sharding import PartitionSpec as P

HEADS = 12
HDIM = 32
PACK = 4
LANES = 128
WIN = 128
LAT = ("zhi", "x", "core")
LON = ("zlo", "y")
ALL = ("zhi", "x", "core", "zlo", "y")


def rings(first):
    order = [(first + i) % 16 for i in range(16)]
    return [
        [(((z // 8 * 4 + x) * 2 + core) * 8 + z % 8) * 4 + y for z in order]
        for x in range(4)
        for core in range(2)
        for y in range(4)
    ]


RINGS = rings(7)
PLANES = [
    [(((z // 8 * 4 + (x + 3 * core) % 4) * 2 + core) * 8 + z % 8) * 4 + y for x in range(4) for y in range(4)]
    for z in range(16)
    for core in range(2)
]
F32 = jnp.float32
BF16 = jnp.bfloat16
LONG = 3 * 10**10


def dot(left, right):
    return jnp.dot(left, right, preferred_element_type=F32)


def dot_nt(left, right):
    return lax.dot_general(left, right, (((1,), (1,)), ((), ())), preferred_element_type=F32)


class Fetch:
    def __init__(self, ref, spot, sem):
        self.spot, self.copy = spot, pltpu.make_async_copy(ref, spot, sem)

    def get(self):
        self.copy.wait()
        return self.spot


def call(kernel, outs, *args, scalars=(), far=(), scratch=(), limit=40, flops=0, spaces=None, after=()):
    n_after = len(after)
    n_scalars, n_far, n_args, n_outs = len(scalars), len(far), len(args), len(outs)

    def body(*refs):
        head, rest = refs[:n_scalars], refs[n_scalars:]
        sources, rest = rest[:n_far], rest[n_far:]
        near, rest = rest[:n_args], rest[n_args + n_after :]
        results, rest = rest[:n_outs], rest[n_outs:]
        if not n_far:
            return kernel(*head, *near, *results, *rest)
        spots, sems, own = rest[:n_far], rest[n_far], rest[n_far + 1 :]
        fetches = [Fetch(sources[i], spots[i], sems.at[i]) for i in range(n_far)]
        for fetch in fetches:
            fetch.copy.start()
        kernel(*head, *fetches, *near, *results, *own)

    specs = [pl.BlockSpec(memory_space=pltpu.SMEM)] * n_scalars
    specs += [pl.BlockSpec(memory_space=pltpu.HBM)] * n_far
    specs += [pl.BlockSpec(memory_space=pltpu.VMEM)] * n_args
    specs += [pl.BlockSpec(memory_space=pl.ANY)] * n_after
    spots = [pltpu.VMEM(a.shape, a.dtype) for a in far]
    if far:
        spots.append(pltpu.SemaphoreType.DMA((n_far,)))
    return pl.pallas_call(
        body,
        out_shape=[jax.ShapeDtypeStruct(s, d) for s, d in outs],
        in_specs=specs,
        out_specs=[pl.BlockSpec(memory_space=space) for space in spaces or [pltpu.VMEM] * n_outs],
        scratch_shapes=spots + list(scratch),
        compiler_params=pltpu.CompilerParams(vmem_limit_bytes=limit * 1024 * 1024),
        name=kernel.__name__,
        cost_estimate=pl.CostEstimate(flops=flops, bytes_accessed=0, transcendentals=0) if flops else None,
    )(*scalars, *far, *args, *after)


PICK = slice(0, 288)
PUT = 256
EDGE_PICK = slice(128, 288)
EDGE_PUT = 544


def constants():
    pick = np.zeros((2 * WIN, 288), np.float32)
    back = np.zeros((288, 2 * WIN), np.float32)
    edge = np.zeros((WIN, 160), np.float32)
    edge_back = np.zeros((160, WIN), np.float32)
    for w in range(2):
        for level in range(2):
            for r in range(8):
                for c in range(8):
                    col, row, below = 4 + 8 * w + c, r % 4, r // 4
                    token = w * WIN + level * 64 + r * 8 + c
                    corner = level * 16 + row * 4 + col - 16
                    grid = level * 64 + row * 16 + col
                    if col >= 16:
                        pick[token, (224 if below else 256) + corner] = 1
                        back[(224 if below else 256) + corner, token] = 1
                    elif below:
                        inner = level * 48 + row * 12 + col - 4
                        pick[token, 128 + inner] = 1
                        back[128 + inner, token] = 1
                    else:
                        pick[token, grid] = 1
                        back[grid, token] = 1
                    if r < 4:
                        token = w * 64 + level * 32 + r * 8 + c
                        edge[token, 128 + corner if col >= 16 else grid] = 1
                        edge_back[128 + corner if col >= 16 else grid, token] = 1
    packed = np.zeros((704, 384), np.float32)
    packed[0:256, 0:288] = pick[:, 0:288]
    packed[256:544, 0:256] = back
    packed[544:704, 0:128] = edge_back
    packed[544:672, 128:288] = edge
    return packed


def columns_matrix():
    columns = np.zeros((128, 128), np.float32)
    for row in range(8):
        for col in range(16):
            at = row * 4 + col if col < 4 else 32 + row * 12 + col - 4
            columns[at, row * 16 + col] = 1
    return columns


def send_kernel(tok, cot, columns, lat_out, diag_out, lon_out):
    pick = columns.get()[...]
    for i, fetch in enumerate((tok, cot)):
        ref = fetch.get()
        upper = dot(pick, ref[:, 0:4].reshape(WIN, -1)).astype(BF16)
        lower = dot(pick[0:32], ref[:, 4:8].reshape(WIN, -1)).astype(BF16)
        lat_out[i * 96 : (i + 1) * 96] = upper[32:128]
        diag_out[i * 32 : (i + 1) * 32] = upper[0:32]
        lon_out[i * 32 : (i + 1) * 32] = lower
        lon_out[64 + i * 32 : 64 + (i + 1) * 32] = upper[0:32]


def pause_kernel(place, out):
    out[0] = place[0]


def normalized(x):
    centered = x - jnp.mean(x, -1, keepdims=True)
    rstd = lax.rsqrt(jnp.mean(centered * centered, -1, keepdims=True) + 1e-5)
    return centered * rstd, rstd


def half_sums(left, right, out, half, count):
    dim = left.shape[1]
    for at in range(6):
        j = half * 6 + at
        term = dot(left[j // 9, :, 0:count], right[j, 0:count])
        out[at * dim : (at + 1) * dim] = term.astype(BF16)


def window_kernel(
    place, ocean_mask, tok, const, w_qkv, cot, w_out, lat, diag, lon, gain,
    other, left, right, windows,
    packed, d_att,
):
    dim = lat.shape[1]
    lat_index = place[0]
    core = lax.rem(lat_index, 2)
    last_band = (lat_index == ocean_mask.shape[1] - 1).astype(jnp.int32)
    scale = HDIM ** (-0.5)
    gains = gain[...].reshape(1, dim).astype(F32)
    lane = lax.broadcasted_iota(jnp.int32, (1, LANES), 1)
    masks = [(lane // HDIM == h).astype(F32).astype(BF16) for h in range(PACK)]
    key_at = lax.broadcasted_iota(jnp.int32, (WIN, PACK * WIN), 0)
    query_at = lax.broadcasted_iota(jnp.int32, (WIN, PACK * WIN), 1) % WIN

    def project(x, g, first):
        rows = slice(first, first + x.shape[0])
        windows[rows] = x.astype(BF16)
        normed = normalized(x)[0] * gains
        left[0, :, rows] = normed.T.astype(BF16)
        packed[rows] = dot(normed.astype(BF16), w_qkv[...]).astype(BF16)
        d_att[rows] = dot_nt(g, w_out[...]).astype(BF16)
        for j in range(dim // LANES):
            right[9 + j, rows] = g[:, j * LANES : (j + 1) * LANES]

    def attend(first, differ):
        rows = slice(first, first + WIN)
        for group in range(HEADS // PACK):
            cols = [slice(p * dim + group * LANES, p * dim + (group + 1) * LANES) for p in range(3)]
            query, keys, values = packed[rows, cols[0]], packed[rows, cols[1]], packed[rows, cols[2]]
            d_out = d_att[rows, cols[0]]
            query_heads = jnp.concatenate([query * m for m in masks], 0)
            d_out_heads = jnp.concatenate([d_out * m for m in masks], 0)
            scores = jnp.where(differ, -1e30, dot_nt(keys, query_heads) * scale)
            expo = jnp.exp(scores - jnp.max(scores, 0, keepdims=True))
            probs = expo / jnp.sum(expo, 0, keepdims=True)
            weights = probs.astype(BF16)
            d_probs = dot_nt(values, d_out_heads)
            inner = jnp.sum(d_probs * probs, 0, keepdims=True)
            d_scores = (probs * (d_probs - inner) * scale).astype(BF16)
            values_t = values.T
            keys_t = keys.T
            att_t, d_query_t = [], []
            for h in range(PACK):
                span = slice(h * WIN, (h + 1) * WIN)
                feats = slice(h * HDIM, (h + 1) * HDIM)
                att_t.append(dot(values_t[feats], weights[:, span]))
                d_query_t.append(dot(keys_t[feats], d_scores[:, span]))
            att_rows = slice(group * LANES, (group + 1) * LANES)
            left[1, att_rows, rows] = jnp.concatenate(att_t, 0).astype(BF16)
            right[group, rows] = jnp.concatenate(d_query_t, 0).T.astype(BF16)
            right[3 + group, rows] = dot(d_scores, query_heads).astype(BF16)
            right[6 + group, rows] = dot(weights, d_out_heads).astype(BF16)

    def sources(i, ref):
        return jnp.concatenate(
            [
                ref[:, 4:8].reshape(WIN, dim),
                lat[i * 96 : (i + 1) * 96],
                diag[i * 32 : (i + 1) * 32],
                lon[i * 32 : (i + 1) * 32],
            ],
            0,
        )

    def edge_sources(i, ref):
        return jnp.concatenate(
            [ref[:, 0:4].reshape(WIN, dim), lon[64 + i * 32 : 64 + (i + 1) * 32]], 0
        )

    def assembled(matrix, tokens, cotangents):
        both = dot(matrix, jnp.concatenate([tokens, cotangents], 1))
        return both[:, 0:dim], both[:, dim : 2 * dim]

    def ocean(band, rows, size):
        first = lax.broadcasted_iota(jnp.int32, (rows, 1), 0) < size
        return jnp.where(first, ocean_mask[0, band], ocean_mask[1, band]).astype(F32)

    x, g = assembled(const[0:256, PICK], sources(0, tok), sources(1, cot))
    project(x, (g * ocean(lat_index, 2 * WIN, WIN)).astype(BF16), 0)
    lower_differs = ((key_at // 8 % 8 >= 4) != (query_at // 8 % 8 >= 4)).astype(jnp.int32)
    for w in range(2):
        attend(w * WIN, lower_differs * last_band > 0)

    @pl.when(lat_index == 0)
    def _():
        last = ocean_mask.shape[1] - 1
        matrix = const[EDGE_PUT : EDGE_PUT + WIN, EDGE_PICK]
        edge_x, edge_g = assembled(matrix, edge_sources(0, tok), edge_sources(1, cot))
        project(edge_x, (edge_g * ocean(last, WIN, 64)).astype(BF16), 2 * WIN)
        attend(2 * WIN, key_at // 64 != query_at // 64)
        half_sums(left, right, other, 1 - core, 3 * WIN)

    @pl.when(lat_index != 0)
    def _():
        half_sums(left, right, other, 1 - core, 2 * WIN)


def branch_kernel(place, left, right, windows, const, w_qkv, gain, mine, own_back, lat_back, side_back, edge_back):
    dim = windows.shape[1]
    lat_index = place[0]
    core = lax.rem(lat_index, 2)
    gains = gain[...].reshape(1, dim).astype(F32)

    def branch(first, count):
        rows = slice(first, first + count)
        xhat, rstd = normalized(windows[rows].astype(F32))
        d_packed = jnp.concatenate([right[j, rows] for j in range(9)], 1)
        d_normed = dot_nt(d_packed, w_qkv[...])
        d_hat = d_normed * gains
        d_branch = rstd * (
            d_hat
            - jnp.mean(d_hat, -1, keepdims=True)
            - xhat * jnp.mean(d_hat * xhat, -1, keepdims=True)
        )
        return d_branch.astype(BF16)

    @pl.when(lat_index == 0)
    def _():
        half_sums(left, right, mine, core, 3 * WIN)
        edge_back[...] = dot(const[EDGE_PUT : EDGE_PUT + 160, 0:128], branch(2 * WIN, WIN)).astype(BF16)

    @pl.when(lat_index != 0)
    def _():
        half_sums(left, right, mine, core, 2 * WIN)
        edge_back[...] = jnp.zeros_like(edge_back)

    back = dot(const[PUT : PUT + 288, 0:256], branch(0, 2 * WIN)).astype(BF16)
    own_back[...] = back[0:128]
    lat_back[...] = back[128:224]
    side_back[0:64] = back[224:288]
    side_back[64:96] = edge_back[128:160]


def add_kernel(mine, received, out):
    out[...] = (mine[...].astype(F32) + received[...].astype(F32)).astype(BF16)


def join_kernel(lat_back, side, out):
    out[0:96] = lat_back[...]
    out[96:128] = side[0:32]


def token_kernel(cot, spread, own, edge, lat, side, out):
    cot, fill = cot.get(), spread.get()[...]
    lower = own[...].astype(F32) + dot(fill[:, 0:32], side[32:64])
    upper = (
        edge[0:128].astype(F32)
        + dot(fill[:, 0:32], lat[96:128] + side[64:96])
        + dot(fill[:, 128:224], lat[0:96])
    )
    shape = (2, 4) + cot.shape[2:]
    out[:, 0:4] = (cot[:, 0:4].astype(F32) + upper.reshape(shape)).astype(BF16)
    out[:, 4:8] = (cot[:, 4:8].astype(F32) + lower.reshape(shape)).astype(BF16)


def result_kernel(place, w_qkv, mine, other, gain, qkv_out, out_out, gain_out):
    dim = out_out.shape[0]
    w_qkv = w_qkv.get()

    def write(halves):
        along = jnp.zeros((dim, LANES), F32)
        for j in range(12):
            at = (j % 6) * dim
            block = halves[j // 6][at : at + dim]
            if j < 9:
                cols = slice(j * LANES, (j + 1) * LANES)
                qkv_out[:, cols] = block
                along = along + w_qkv[:, cols].astype(F32) * block.astype(F32)
            else:
                out_out[:, (j - 9) * LANES : (j - 8) * LANES] = block
        total = jnp.sum(along.T, 0, keepdims=True)
        gains = gain[...].reshape(1, dim).astype(F32)
        gain_out[...] = (total / gains).astype(BF16).reshape(dim)

    core = lax.rem(place[0], 2)

    @pl.when(core == 0)
    def _():
        write((mine, other))

    @pl.when(core != 0)
    def _():
        write((other, mine))


def exchange(parts, groups):
    return lax.all_to_all(parts, ALL, 0, 0, axis_index_groups=groups, tiled=False)


def summed(parts):
    return jnp.sum(parts.astype(F32), 0).astype(BF16)


def copies(part):
    return jnp.broadcast_to(part[None], (16,) + part.shape)


def swapped(array):
    return lax.ppermute(array, "core", [(0, 1), (1, 0)])


def tied(*arrays):
    return lax.optimization_barrier(arrays)


def local(tokens, cotangent, ocean_mask, gain, w_qkv, w_out):
    dim = w_out.shape[0]
    n_lat, n_lon = lax.axis_size(LAT), lax.axis_size(LON)
    place = lax.axis_index(LAT).astype(jnp.int32).reshape(1)
    constant = functools.partial(jnp.asarray, dtype=BF16)
    columns = columns_matrix()
    spread = np.zeros((128, 256), np.float32)
    spread[:, 0:32], spread[:, 128:224] = columns[0:32].T, columns[32:128].T

    def place_of(a, b):
        return a * n_lon + b % n_lon

    south = [(a, a + 1) for a in range(n_lat - 1)]
    diagonal = [(place_of(a, b), place_of(a + 1, b + 1)) for a in range(n_lat - 1) for b in range(n_lon)]
    east = [(b, (b + 1) % n_lon) for b in range(n_lon)]

    def back(pairs):
        return [(target, source) for source, target in pairs]

    lat, diag, lon = call(
        send_kernel, [((192, dim), BF16), ((64, dim), BF16), ((128, dim), BF16)],
        far=(tokens, cotangent, constant(columns)), limit=60,
    )
    lat = lax.ppermute(lat, LAT, back(south))
    diag = lax.ppermute(diag, LAT + LON, back(diagonal))
    lon = lax.ppermute(lon, LON, back(east))
    near = (tokens, constant(constants()), w_qkv, cotangent, w_out)
    (pause,) = call(pause_kernel, [((1,), jnp.int32)], scalars=(place,), limit=8, flops=LONG, spaces=[pltpu.SMEM])
    half = 6 * dim
    shapes = [(half, LANES), (2, dim, 3 * WIN), (12, 3 * WIN, LANES), (3 * WIN, dim)]
    other, left, right, windows = call(
        window_kernel, [(shape, BF16) for shape in shapes],
        *near, lat, diag, lon, gain,
        scalars=(place, ocean_mask.T), after=(pause,),
        scratch=[pltpu.VMEM((3 * WIN, 3 * dim), BF16), pltpu.VMEM((3 * WIN, dim), BF16)],
    )
    shapes = [(half, LANES), (WIN, dim), (96, dim), (96, dim), (160, dim)]
    mine, own_back, lat_back, side_back, edge_back = call(
        branch_kernel, [(shape, BF16) for shape in shapes],
        left, right, windows, near[1], w_qkv, gain,
        scalars=(place,), flops=LONG,
    )

    side = lax.ppermute(side_back, LON, east)
    (mine,) = call(add_kernel, [((half, LANES), BF16)], mine, swapped(other))
    mine = summed(exchange(mine.reshape(16, half // 16, LANES), PLANES))
    mine = summed(exchange(mine.reshape(16, half // 256, LANES), RINGS))
    (rows_back,) = call(
        join_kernel, [((WIN, dim), BF16)], lat_back, side, flops=LONG
    )
    mine, rows_back = tied(mine, rows_back)
    rows_back = lax.ppermute(rows_back, LAT, south)
    mine = exchange(copies(mine), RINGS).reshape(half // 16, LANES)
    mine = exchange(copies(mine), PLANES).reshape(half, LANES)
    (token_grad,) = call(
        token_kernel, [(tokens.shape, BF16)],
        own_back, edge_back, rows_back, side,
        far=(cotangent, constant(spread)), flops=LONG,
    )
    mine, token_grad = tied(mine, token_grad)
    other = swapped(mine)
    qkv_grad, out_grad, gain_grad = call(
        result_kernel, [(w_qkv.shape, BF16), (w_out.shape, BF16), ((dim,), BF16)],
        mine, other, gain,
        scalars=(place,), far=(w_qkv,),
    )
    return token_grad, qkv_grad, out_grad, gain_grad


def solution(mesh):
    fine = Mesh(mesh.devices.reshape(2, 4, 2, 8, 4), ("zhi", "x", "core", "zlo", "y"))
    tiles = P(None, LAT, LON, None)
    return jax.shard_map(
        local,
        mesh=fine,
        in_specs=(tiles, tiles, P(None, LON), P(), P(), P()),
        out_specs=(tiles, P(), P(), P()),
        check_vma=False,
    )
```
